32 devices in a mesh: row: 8 (over z, y), col: 4 (over x, core).
Axes of the slice: x: 2, y: 2, z: 4, core: 2. Of those that a mesh axis runs over, the one named last changes fastest.
Arguments:
- amplitudes: bfloat16 [4, 1280, 1280], P(None, ('row', 'col')), may hold values from -0.75 to 0.75
- integrals: bfloat16 [24, 1280, 1280], P('row', 'col'), may hold values from -0.15625 to 0.15625
- occupied_integrals: bfloat16 [24, 160, 1280], P('row'), may hold values from -1 to 1
- pair_orbitals: int32 [4, 2], replicated, may hold values from 0 to 159
- amplitude_tiles: int32 [4, 20, 20], replicated, may hold values 0 or 1
- integral_tiles: int32 [20, 20], replicated, may hold values 0 or 1
Outputs:
- residual: float32 [4, 1280, 1280], P(None, 'col', 'row')
The draws below stay inside these ranges and needn't reach their ends.
All inputs are finite; a program needn't handle non-finite values.
Results may differ from the reference program's by a relative error of at most 0.005.
Values may be sent and summed in bfloat16 or wider, within the bound.
No kernel may reach another device: no remote copies, remote signals or barrier semaphores. Data moves between devices by JAX's collectives and lax.ppermute only.
A program may use at most 128 MiB of HBM per device.

```python
import jax
import jax.numpy as jnp
from jax import lax

O = 160
TILE = 64
VT = 20
P_SIZE = 4
V = 1280
NAUX = 24


def place_ends(array, key, least, largest):
    shape = array.shape
    place = [jax.random.randint(jax.random.fold_in(key, axis), (), 0, shape[axis]) for axis in range(len(shape))]
    array = array.at[tuple(place)].set(least)
    longest = shape.index(max(shape))
    place[longest] = (place[longest] + 1) % shape[longest]
    return array.at[tuple(place)].set(largest)


def block_levels(stream_key, shape, shards, low, top_value):
    gain, own = 1.0, jax.random.fold_in(stream_key, 6)
    for axis_at, parts in shards:
        heights = jnp.exp(jax.random.uniform(jax.random.fold_in(own, axis_at), (parts,), jnp.float32, low / len(shards), top_value / len(shards)))
        gain = gain * jnp.repeat(heights, shape[axis_at] // parts).reshape([-1 if axis == axis_at else 1 for axis in range(len(shape))])
    return gain


def gaussian(own_key, dims, width, most, pieces=(), kind=jnp.bfloat16):
    values = width * jax.random.normal(own_key, dims, jnp.float32)
    if pieces:
        values = values * block_levels(own_key, dims, pieces, -0.22, 0.18)
    return jnp.clip(values, -most, most).astype(kind)


def setup_inputs(seed: int = 0) -> dict:
    seeds = jax.random.split(jax.random.key(seed), 7)
    return {
        "amplitudes": gaussian(seeds[0], (P_SIZE, V, V), 0.125, 0.75, ((1, 32),)),
        "integrals": gaussian(seeds[1], (NAUX, V, V), V ** -0.5, 0.15625, ((0, 8), (1, 4))),
        "occupied_integrals": gaussian(seeds[2], (NAUX, O, V), 0.17, 1.0, ((0, 8),)),
        "pair_orbitals": place_ends(jax.random.randint(seeds[3], (P_SIZE, 2), 0, O), jax.random.fold_in(seeds[3], 1), 0, O - 1).astype(jnp.int32),
        "amplitude_tiles": place_ends((jax.random.randint(seeds[4], (P_SIZE, VT, VT), 0, 2) < 1).astype(jnp.int32), jax.random.fold_in(seeds[4], 1), 0, 1),
        "integral_tiles": place_ends((jax.random.randint(seeds[5], (VT, VT), 0, 4) < 3).astype(jnp.int32), jax.random.fold_in(seeds[5], 1), 0, 1),
    }


def expand_tiles(tiles, tile_size):
    return jnp.repeat(jnp.repeat(tiles, tile_size, axis=-2), tile_size, axis=-1)


def reference(amplitudes, integrals, occupied_integrals, pair_orbitals, amplitude_tiles, integral_tiles):
    masked_amp = amplitudes * expand_tiles(amplitude_tiles, TILE).astype(jnp.bfloat16)
    masked_int = integrals * expand_tiles(integral_tiles, TILE).astype(jnp.bfloat16)[None]
    amp_wide = masked_amp.astype(jnp.float32)

    def one_aux(total, factor):
        factor_wide = factor.astype(jnp.float32)
        inter = jnp.einsum('ac,pcd->pad', factor_wide, amp_wide).astype(jnp.bfloat16)
        term = jnp.einsum('pad,bd->pab', inter.astype(jnp.float32), factor_wide)
        return total + term, None

    ladder, _ = lax.scan(one_aux, jnp.zeros((P_SIZE, V, V), jnp.float32), masked_int)
    orbital_ids = jnp.arange(O, dtype=jnp.int32)
    pick_first = (pair_orbitals[:, 0][:, None] == orbital_ids[None, :]).astype(jnp.float32)
    pick_second = (pair_orbitals[:, 1][:, None] == orbital_ids[None, :]).astype(jnp.float32)
    occ_wide = occupied_integrals.astype(jnp.float32)
    first_rows = jnp.einsum('po,qov->qpv', pick_first, occ_wide)
    second_rows = jnp.einsum('po,qov->qpv', pick_second, occ_wide)
    carried = jnp.einsum('qpc,pcd->qpd', second_rows, amp_wide)
    cycle = jnp.einsum('qpa,qpb->pab', first_rows, carried)
    return ladder + cycle
```

```python
import functools

import jax
import jax.numpy as jnp
from jax import lax
from jax.experimental import pallas as pl
from jax.experimental.pallas import tpu as pltpu
from jax.sharding import PartitionSpec as P

TILE = 64
BF = jnp.bfloat16
F32 = jnp.float32
VMEM = pl.BlockSpec(memory_space=pltpu.VMEM)
SMEM = pl.BlockSpec(memory_space=pltpu.SMEM)
LIMIT = 30 * 2**20


def kernel_call(body, outs, ins, scratch=(), flops=0, nbytes=0, name=None):
    return pl.pallas_call(
        body,
        out_shape=outs,
        in_specs=[SMEM] + [VMEM] * (len(ins) - 1),
        out_specs=jax.tree.map(lambda _: VMEM, outs),
        scratch_shapes=scratch,
        compiler_params=pltpu.CompilerParams(vmem_limit_bytes=LIMIT),
        cost_estimate=pl.CostEstimate(flops=flops, bytes_accessed=nbytes, transcendentals=0),
        name=name,
    )(*ins)


def like(shape, dtype):
    return jax.ShapeDtypeStruct(shape, dtype)


def place_blocks(order, ids, *refs):
    blocks, out = refs[:-1], refs[-1]
    for place, block in zip(order(ids), blocks, strict=True):
        out[place] = block[...]


def carried_terms(width, ids, second, amp, out):
    u = jnp.dot(second[...], amp[...], preferred_element_type=F32)
    high = u.astype(BF)
    low = (u - high.astype(F32)).astype(BF)
    both = jnp.concatenate([high.astype(F32)[:width], low.astype(F32)[:width]], axis=0)
    out[...] = both.T.astype(BF)


def segments(chunk, width, rows):
    found, at, end, to = [], chunk * width, (chunk + 1) * width, 0
    while at < end:
        piece, low = divmod(at, rows)
        count = min(rows - low, end - at)
        found.append((piece, low, count, to))
        at, to = at + count, to + count
    return found


def partial_sums(chunk, width, pieces, aux, block, ids, *refs):
    factors = [refs[j * aux : (j + 1) * aux] for j in range(pieces)]
    amp, carried, first, keep, send, picked, inter, total = refs[pieces * aux :]
    rows = factors[0][0].shape[0]
    size = amp.shape[1]
    col, low = ids[0], ids[1]
    for piece, start, count, to in segments(chunk, width, rows):
        for q in range(aux):
            picked[pl.ds(q * width + to, count), :] = factors[piece][q][start : start + count, :]

    step = 256 if size % 256 == 0 else size

    def columns(i, _):
        at = pl.ds(pl.multiple_of(i * step, step), step)
        inter[:, at] = jnp.dot(picked[...], amp[:, at], preferred_element_type=F32).astype(BF)
        return 0

    lax.fori_loop(0, size // step, columns, 0)
    for j in range(pieces):
        at = pl.ds(pl.multiple_of((col ^ j) * rows, 16), rows)
        value = jnp.dot(carried[at, :], first[...], preferred_element_type=F32)
        for q in range(aux):
            value += lax.dot_general(
                factors[j][q][...],
                inter[pl.ds(q * width, width), :],
                (((1,), (1,)), ((), ())),
                preferred_element_type=F32,
            )
        total[at, :] = value
    for h in range(keep.shape[0]):
        mine = pl.multiple_of((2 * h + low) * block, 8)
        theirs = pl.multiple_of((2 * h + 1 - low) * block, 8)
        keep[h] = total[pl.ds(mine, block), :]
        send[h] = total[pl.ds(theirs, block), :].astype(BF)


def add_and_split(ids, keep, got, own, *messages):
    high = ids[2]
    own[...] = keep[high] + got[high].astype(F32)
    for k, message in enumerate(messages, 1):
        message[...] = (keep[high ^ k] + got[high ^ k].astype(F32)).astype(BF)


def add_up(ids, own, *refs):
    value = own[...]
    for got in refs[:-1]:
        value += got[...].astype(F32)
    refs[-1][...] = value


def finish(ids, *refs):
    out = refs[-1]
    for k, part in enumerate(refs[:-1]):
        out[ids[0] ^ k] = part[...].T


def local(n_row, n_col, amplitudes, integrals, occupied, pairs, amp_tiles, int_tiles):
    n_pair, chunk_rows, size = amplitudes.shape
    aux, piece_rows, _ = integrals.shape
    n_high = n_row // 2
    block = size // n_row
    col, row = lax.axis_index("col"), lax.axis_index("row")
    low, high = row % 2, row // 2
    ids = jnp.stack([col, low, high, row]).astype(jnp.int32)

    def over_col(x, k):
        return lax.ppermute(x, "col", [(i, i ^ k) for i in range(n_col)])

    def over_low(x):
        return lax.ppermute(x, "row", [(i, i ^ 1) for i in range(n_row)])

    def over_high(x, k):
        return lax.ppermute(x, "row", [(i, (i // 2 ^ k) * 2 + i % 2) for i in range(n_row)])

    def up(x):
        return lax.ppermute(x, "row", [(i, (i + 2) % n_row) for i in range(n_row)])

    tiles_here = piece_rows // TILE
    own_tiles = lax.dynamic_slice_in_dim(int_tiles, col * tiles_here, tiles_here, 0)
    int_mask = jnp.repeat(jnp.repeat(own_tiles.astype(BF), TILE, axis=0), TILE, axis=1)
    factors = [None] * n_col
    factors[0] = [integrals[q] * int_mask for q in range(aux)]
    factors[2] = [over_col(x, 2) for x in factors[0]]
    factors[1] = [over_col(x, 1) for x in factors[0]]
    factors[3] = [over_col(x, 1) for x in factors[2]]

    tile_of = ((row * n_col + col) * chunk_rows + jnp.arange(chunk_rows, dtype=jnp.int32)) // TILE
    picker = (tile_of[:, None] == jnp.arange(amp_tiles.shape[1], dtype=jnp.int32)[None, :]).astype(BF)
    row_mask = jnp.einsum("nk,pkm->pnm", picker, amp_tiles.astype(BF))
    masked = amplitudes * jnp.repeat(row_mask, TILE, axis=2)
    mine = [lax.dynamic_index_in_dim(masked, col ^ k, 0, keepdims=False) for k in range(n_col)]
    mine = [mine[0]] + [over_col(mine[k], k) for k in range(1, n_col)]
    slab = kernel_call(
        functools.partial(place_blocks, lambda ids: [ids[0] ^ k for k in range(n_col)]),
        like((n_col, chunk_rows, size), BF),
        (ids, *mine),
        nbytes=4 * n_col * chunk_rows * size,
        name="own_rows",
    ).reshape(n_col * chunk_rows, size)
    slabs = [slab]
    for _ in range(n_high - 1):
        slabs.append(up(slabs[-1]))
    slabs = slabs + [over_low(x) for x in slabs]

    def slab_places(ids):
        ring = [lax.rem(ids[2] + (n_high - s), n_high) * 2 for s in range(n_high)]
        return [h + ids[1] for h in ring] + [h + 1 - ids[1] for h in ring]

    amp = kernel_call(
        functools.partial(place_blocks, slab_places),
        like((n_row, n_col * chunk_rows, size), BF),
        (ids, *slabs),
        nbytes=4 * size * size,
        name="all_rows",
    ).reshape(size, size)

    pair = lax.dynamic_index_in_dim(pairs, col, 0, keepdims=False)
    first = lax.dynamic_index_in_dim(occupied, pair[0], 1, keepdims=False)
    second = lax.dynamic_index_in_dim(occupied, pair[1], 1, keepdims=False)
    second = jnp.concatenate([second, jnp.zeros((16 - aux, size), BF)], axis=0)
    first = first.reshape(aux, n_col, piece_rows)
    first = jnp.concatenate(
        [lax.dynamic_index_in_dim(first, col ^ k, 1, keepdims=False) for k in range(n_col)], axis=1
    )
    first = jnp.concatenate([first, first], axis=0)
    carried = kernel_call(
        functools.partial(carried_terms, aux),
        like((size, 2 * aux), BF),
        (ids, second, amp),
        flops=32 * size * size,
        nbytes=2 * size * size,
        name="carried",
    )

    width = 256 if size % 256 == 0 else piece_rows
    flat = [x for piece in factors for x in piece]
    sums = []
    for c in range(size // width):
        keep, send = kernel_call(
            functools.partial(partial_sums, c, width, n_col, aux, block),
            (like((n_high, block, width), F32), like((n_high, block, width), BF)),
            (ids, *flat, amp, carried, first[:, c * width : (c + 1) * width]),
            scratch=[
                pltpu.VMEM((aux * width, size), BF),
                pltpu.VMEM((aux * width, size), BF),
                pltpu.VMEM((size, width), F32),
            ],
            flops=4 * aux * width * size * size,
            nbytes=2 * size * size,
            name="partial_sums",
        )
        got = over_low(send)
        own, *messages = kernel_call(
            add_and_split,
            (like((block, width), F32),) + (like((block, width), BF),) * (n_high - 1),
            (ids, keep, got),
            nbytes=10 * n_high * block * width,
            name="add_low",
        )
        messages = [over_high(m, k) for k, m in enumerate(messages, 1)]
        sums.append(
            kernel_call(
                add_up, like((block, width), F32), (ids, own, *messages), nbytes=14 * block * width, name="add_high"
            )
        )
    whole = jnp.concatenate(sums, axis=1)
    parts = [whole[:, k * piece_rows : (k + 1) * piece_rows] for k in range(n_col)]
    parts = [parts[0]] + [over_col(parts[k], k) for k in range(1, n_col)]
    return kernel_call(
        finish, like((n_pair, piece_rows, block), F32), (ids, *parts), nbytes=8 * n_pair * piece_rows * block, name="finish"
    )


def solution(mesh):
    placed = (
        P(None, ("row", "col"), None),
        P("row", "col", None),
        P("row", None, None),
        P(),
        P(),
        P(),
    )
    return jax.shard_map(
        functools.partial(local, mesh.shape["row"], mesh.shape["col"]),
        mesh=mesh,
        in_specs=placed,
        out_specs=P(None, "col", "row"),
        check_vma=False,
    )
```

```python
import functools

import jax
import jax.numpy as jnp
from jax import lax
from jax.experimental import pallas as pl
from jax.experimental.pallas import tpu as pltpu
from jax.sharding import PartitionSpec as P

TILE = 64
BF = jnp.bfloat16
F32 = jnp.float32
VMEM = pl.BlockSpec(memory_space=pltpu.VMEM)
SMEM = pl.BlockSpec(memory_space=pltpu.SMEM)
HBM = pl.BlockSpec(memory_space=pltpu.HBM)
LIMIT = 10 * 2**20
COL, LOW, HIGH, ROW = range(4)


def kernel_call(body, outs, ins, scratch=(), name=None, out_spec=VMEM, aliases=None):
    return pl.pallas_call(
        body,
        out_shape=outs,
        in_specs=[SMEM] + [VMEM] * (len(ins) - 1),
        out_specs=jax.tree.map(lambda _: out_spec, outs),
        scratch_shapes=scratch,
        compiler_params=pltpu.CompilerParams(vmem_limit_bytes=LIMIT),
        cost_estimate=pl.CostEstimate(flops=0, bytes_accessed=0, transcendentals=0),
        input_output_aliases=aliases or {},
        name=name,
    )(*ins)


def like(shape, dtype):
    return jax.ShapeDtypeStruct(shape, dtype)


class Box:
    def __init__(self, value):
        self.value = value


def tie(*boxes):
    values = lax.optimization_barrier(tuple(box.value for box in boxes))
    for box, value in zip(boxes, values, strict=True):
        box.value = value


def iota(shape, dim):
    return lax.broadcasted_iota(jnp.int32, shape, dim)


def spread(row_tiles, tiles, size):
    count = tiles.shape[0]
    picker = (row_tiles == iota((row_tiles.shape[0], count), 1)).astype(F32).astype(BF)
    wide = (iota((count, size), 1) // TILE == iota((count, size), 0)).astype(F32).astype(BF)
    rows = jnp.dot(picker, tiles.astype(F32).astype(BF), preferred_element_type=F32).astype(BF)
    return jnp.dot(rows, wide, preferred_element_type=F32).astype(BF)


def mask_slab(n_col, ks, ids, tiles, *refs):
    pieces, out = refs[:-1], refs[-1]
    rows, size = pieces[0].shape
    for k, piece in zip(ks, pieces, strict=True):
        owner = ids[COL] ^ k
        row_tiles = ((ids[ROW] * n_col + owner) * rows + iota((rows, 1), 0)) // TILE
        out[owner % 2] = piece[...] * spread(row_tiles, tiles[...], size)


def place_blocks(places, ids, *refs):
    blocks, out = refs[:-1], refs[-1]
    for place, block in zip(places(ids), blocks, strict=True):
        out[place] = block[...]


def masked_block(ids, tiles, piece, group, half, groups, block, size):
    first = ((piece * groups + group) * 2 + half) * block
    return spread((first + iota((block, 1), 0)) // TILE, tiles[...], size)


def place_pieces(ks, ids, tiles, *refs):
    pieces, (other, kept) = refs[: len(ks)], refs[len(ks) :]
    for k, piece in zip(ks, pieces, strict=True):
        aux, groups, _, block, size = piece.shape
        owner = ids[COL] ^ k
        for half, out in ((1 - ids[LOW], other), (ids[LOW], kept)):
            for g in range(groups):
                mask = masked_block(ids, tiles, owner, g, half, groups, block, size)
                for q in range(aux):
                    out[q, owner * groups + g] = piece[q, g, half] * mask


def place_halves(ks, other_half, ids, tiles, *refs):
    pieces, out = refs[: len(ks)], refs[-1]
    half = 1 - ids[LOW] if other_half else ids[LOW]
    for k, piece in zip(ks, pieces, strict=True):
        aux, groups, block, size = piece.shape
        owner = ids[COL] ^ k
        for g in range(groups):
            mask = masked_block(ids, tiles, owner, g, half, groups, block, size)
            for q in range(aux):
                out[q, owner * groups + g] = piece[q, g] * mask


def multiply_rows(factors, inter, carried, first, width):
    value = jnp.dot(carried[...], first[...], preferred_element_type=F32)
    for q in range(factors.shape[0]):
        value += lax.dot_general(
            factors[q],
            inter[pl.ds(q * width, width), :],
            (((1,), (1,)), ((), ())),
            preferred_element_type=F32,
        )
    return value


def runs(segments, block):
    found, to = [], 0
    for piece, start, count in segments:
        end = start + count
        while start < end:
            group, half, at = start // (2 * block), start // block % 2, start % block
            n = min(block - at, end - start)
            found.append((piece, group, half, at, n, to))
            start, to = start + n, to + n
    return found


def pick_rows(segments, width, ids, other, kept, picked):
    aux, n_high, block, _ = other.shape
    groups = max(1, n_high // 4)
    for low in range(2):

        @pl.when(ids[LOW] == low)
        def _():
            for piece, group, half, at, n, to in runs(segments, block):
                source = kept if half == low else other
                for q in range(aux):
                    picked[q * width + to : q * width + to + n, :] = source[
                        q, (ids[COL] ^ piece) * groups + group, at : at + n, :
                    ]


def times_amplitudes(picked, amp, inter, more=None):
    size = amp.shape[1]
    step = 256 if size % 256 == 0 else size
    rows = inter.shape[0]
    for i in range(size // step):
        at = slice(i * step, (i + 1) * step)
        value = jnp.dot(picked[...], amp[:, at], preferred_element_type=F32)
        inter[:, at] = value[:rows].astype(BF)
        if more is not None:
            more[:, at] = value[rows:]


def first_send_part(segments, width, ids, *refs):
    others, kepts, amp, factors, second, first, inter, send, other, kept, picked, rows, turned = refs
    aux = factors.shape[0]
    block = send.shape[1]
    pick_rows(segments, width, ids, others, kepts, picked)
    picked[aux * width :, :] = second[...]
    times_amplitudes(picked, amp, inter, rows)
    u = rows[...]
    high = u.astype(BF).astype(F32)
    turned[...] = jnp.concatenate([high[:aux], (u - high)[:aux]], axis=0).T
    for h in range(send.shape[0]):
        for half, out in ((1 - ids[LOW], other), (ids[LOW], kept)):
            at = pl.ds(pl.multiple_of((2 * h + half) * block, 8), block)
            out[h * block : (h + 1) * block, :] = turned[at, :].astype(BF)
    value = multiply_rows(factors, inter, other, first, width)
    for h in range(send.shape[0]):
        send[h] = value[h * block : (h + 1) * block, :].astype(BF)


def send_part(segments, width, ids, *refs):
    others, kepts, amp, factors, carried, first, inter, send, picked = refs
    block = send.shape[1]
    pick_rows(segments, width, ids, others, kepts, picked)
    times_amplitudes(picked, amp, inter)
    value = multiply_rows(factors, inter, carried, first, width)
    for h in range(send.shape[0]):
        send[h] = value[h * block : (h + 1) * block, :].astype(BF)


def keep_rows(count, width, ids, factors, carried, *refs):
    inter, first, got = refs[:count], refs[count : 2 * count], refs[2 * count : 3 * count]
    total = refs[-1]
    block = got[0].shape[1]
    for c in range(count):
        value = multiply_rows(factors, inter[c], carried, first[c], width)
        for h in range(got[c].shape[0]):
            total[h, :, c * width : (c + 1) * width] = (
                value[h * block : (h + 1) * block, :] + got[c][h].astype(F32)
            )
    return refs[3 * count : -1], total


def keep_direct(count, width, ids, *refs):
    (own, *messages), total = keep_rows(count, width, ids, *refs)
    own[...] = total[ids[HIGH]]
    for k, message in enumerate(messages, 1):
        message[...] = total[ids[HIGH] ^ k].astype(BF)


def keep_halves(count, width, ids, *refs):
    (mine, message), total = keep_rows(count, width, ids, *refs)
    for i in range(mine.shape[0]):
        mine[i] = total[ids[HIGH] ^ (2 * i)]
        message[i] = total[ids[HIGH] ^ (2 * i + 1)].astype(BF)


def add_halves(ids, mine, got, kept, message):
    for i in range(kept.shape[0]):
        kept[i] = mine[2 * i] + got[2 * i].astype(F32)
        message[i] = (mine[2 * i + 1] + got[2 * i + 1].astype(F32)).astype(BF)


def add_up(ids, own, *refs):
    value = own[...]
    for got in refs[:-1]:
        value += got[...].astype(F32)
    refs[-1][...] = value


def finish(places, ids, *refs):
    parts, out, whole, sems = refs[:-3], refs[-3], refs[-2], refs[-1]
    copies = []
    for k in range(whole.shape[0]):
        for (piece, start, count), part in zip(places, parts, strict=True):
            if piece == k:
                whole[k, :, start : start + count] = part[...]
        copy = pltpu.make_async_copy(whole.at[k], out.at[ids[COL] ^ k], sems.at[k])
        copy.start()
        copies.append(copy)
    for copy in copies:
        copy.wait()


def local(n_row, n_col, amplitudes, integrals, occupied, pairs, amp_tiles, int_tiles):
    n_pair, chunk_rows, size = amplitudes.shape
    aux, piece_rows, _ = integrals.shape
    n_high = n_row // 2
    block = size // n_row
    groups = piece_rows // (2 * block)
    half_size = n_high * block
    col, row = lax.axis_index("col"), lax.axis_index("row")
    ids = jnp.stack([col, row % 2, row // 2, row]).astype(jnp.int32)

    def over_col(x, k):
        return lax.ppermute(x, "col", [(i, i ^ k) for i in range(n_col)])

    def over_low(x):
        return lax.ppermute(x, "row", [(i, i ^ 1) for i in range(n_row)])

    def over_high(x, k):
        return lax.ppermute(x, "row", [(i, (i // 2 ^ k) * 2 + i % 2) for i in range(n_row)])

    def up(x):
        return lax.ppermute(x, "row", [(i, (i + 2) % n_row) for i in range(n_row)])

    mine = [lax.dynamic_index_in_dim(amplitudes, col ^ k, 0, keepdims=False) for k in range(n_col)]
    mine = [Box(mine[0])] + [Box(over_col(mine[k], k)) for k in range(1, n_col)]
    split = integrals.reshape(aux, groups, 2, block, size)
    low = row % 2
    other, kept = {}, {}
    send_other = Box(lax.dynamic_index_in_dim(split, 1 - low, 2, keepdims=False))
    send_kept = Box(lax.dynamic_index_in_dim(split, low, 2, keepdims=False))
    split1 = Box(over_col(integrals, 1))
    tie(send_other, send_kept, split1, *mine[1:])
    other[2] = Box(over_col(send_other.value, 2))
    pair_tiles = lax.dynamic_index_in_dim(amp_tiles, col, 0, keepdims=False)

    def half_slab(ks):
        return kernel_call(
            functools.partial(mask_slab, n_col, ks),
            like((2, chunk_rows, size), BF),
            (ids, pair_tiles, *[mine[k].value for k in ks]),
            name="half_slab",
        ).reshape(2 * chunk_rows, size)

    rings = [[Box(half_slab((0, 1)))], [Box(half_slab((2, 3)))]]
    swapped = [[], []]
    for s in range(n_high):
        for r, ring in enumerate(rings):
            if s > 0:
                tie(ring[s], swapped[r][-1])
            if s + 1 < n_high:
                ring.append(Box(up(ring[s].value)))
            swapped[r].append(Box(over_low(ring[s].value)))
    tie(other[2], rings[0][-1], rings[1][-2], swapped[0][-3], swapped[1][-3])
    tie(send_kept, other[2])
    other[3] = Box(over_col(other[2].value, 1))
    kept[2] = Box(over_col(send_kept.value, 2))

    def slab_places(ids):
        highs = [lax.rem(ids[HIGH] + (n_high - s), n_high) for s in range(n_high)]
        side = ids[COL] // 2
        return [
            ((h * 2 + low) * 2) + (side ^ r)
            for low in (ids[LOW], 1 - ids[LOW])
            for r in range(2)
            for h in highs
        ]

    slabs = rings[0] + rings[1] + swapped[0] + swapped[1]
    amp = kernel_call(
        functools.partial(place_blocks, slab_places),
        like((n_row * 2, 2 * chunk_rows, size), BF),
        (ids, *[slab.value for slab in slabs]),
        name="all_rows",
    )
    amp = Box(amp.reshape(size, size))

    shape = like((aux, n_high, block, size), BF)
    all_other, all_kept = kernel_call(
        functools.partial(place_pieces, (0, 1)),
        (shape, shape),
        (ids, int_tiles, split, split1.value.reshape(split.shape)),
        name="place_pieces",
    )

    def place(pieces, into, other_half):
        return kernel_call(
            functools.partial(place_halves, (2, 3), other_half),
            shape,
            (ids, int_tiles, pieces[2].value, pieces[3].value, into),
            aliases={4: 0},
            name="place_halves",
        )

    def flat(x):
        return x.reshape(aux, half_size, size)

    all_other = place(other, all_other, True)
    all_kept = Box(all_kept)

    orbitals = jnp.arange(occupied.shape[1], dtype=jnp.int32)
    picks = (pairs.T.reshape(-1)[:, None] == orbitals[None, :]).astype(BF)
    rows = jnp.einsum("po,qov->pqv", picks, occupied, preferred_element_type=F32).astype(BF)
    first = lax.dynamic_index_in_dim(rows, col, 0, keepdims=False)
    second = lax.dynamic_index_in_dim(rows, col + n_pair, 0, keepdims=False)
    second = jnp.concatenate([second, jnp.zeros((16 - aux, size), BF)], axis=0)
    first = first.reshape(aux, n_col, piece_rows)
    first = [lax.dynamic_index_in_dim(first, col ^ k, 1, keepdims=False) for k in range(n_col)]
    first = [jnp.concatenate([x, x], axis=0) for x in first]

    width = 256 if size % 256 == 0 else piece_rows
    cut = 2 * width - piece_rows
    rest = piece_rows - cut
    order = [(1, 0, piece_rows), (0, 0, cut), (2, 0, piece_rows), (3, 0, cut), (3, cut, rest), (0, cut, rest)]
    chunks, where, at = [], [], 0
    for piece, start, count in order:
        spans = []
        while count:
            if at % width == 0:
                chunks.append([])
            n = min(count, width - at % width)
            chunks[-1].append((piece, start, n))
            spans.append((at // width, at % width, n))
            start, count, at = start + n, count - n, at + n
        where.append(spans)
    first = [jnp.concatenate([first[p][:, s : s + n] for p, s, n in chunk], axis=1) for chunk in chunks]

    inter, got, sums, carried = {}, {}, {}, []

    def send_chunk(c):
        pieces = (all_other, all_kept.value)
        outs = (like((aux * width, size), BF), like((n_high, block, width), BF))
        if not carried:
            extra = second.shape[0]
            x, send, *terms = kernel_call(
                functools.partial(first_send_part, chunks[c], width),
                outs + (like((half_size, 2 * aux), BF),) * 2,
                (ids, *pieces, amp.value, flat(all_other), second, first[c]),
                scratch=[
                    pltpu.VMEM((aux * width + extra, size), BF),
                    pltpu.VMEM((extra, size), F32),
                    pltpu.VMEM((size, 2 * aux), F32),
                ],
                name="send_part",
            )
            carried.extend(terms)
        else:
            x, send = kernel_call(
                functools.partial(send_part, chunks[c], width),
                outs,
                (ids, *pieces, amp.value, flat(all_other), carried[0], first[c]),
                scratch=[pltpu.VMEM((aux * width, size), BF)],
                name="send_part",
            )
        inter[c] = Box(x)
        got[c] = Box(over_low(send))

    def keep_chunks(cs, direct=False):
        n = len(cs)
        wide = n * width
        half = n_high // 2
        if direct:
            body, outs = keep_direct, (like((block, wide), F32),) + (like((block, wide), BF),) * (n_high - 1)
        else:
            body, outs = keep_halves, (like((half, block, wide), F32), like((half, block, wide), BF))
        own, *messages = kernel_call(
            functools.partial(body, n, width),
            outs,
            (ids, flat(all_kept.value), carried[1])
            + tuple(inter[c].value for c in cs)
            + tuple(first[c] for c in cs)
            + tuple(got[c].value for c in cs),
            scratch=[pltpu.VMEM((n_high, block, wide), F32)],
            name="keep_part",
        )
        if direct:
            messages = [Box(over_high(m, k)) for k, m in enumerate(messages, 1)]
        else:
            messages = [Box(over_high(messages[0], 1))]
        return Box(own), messages

    def add_stages(own, messages):
        step = 2
        while own.value.shape[0] > 1:
            half = own.value.shape[0] // 2
            shape = (half,) + own.value.shape[1:]
            mine, message = kernel_call(
                add_halves, (like(shape, F32), like(shape, BF)), (ids, own.value, messages[0].value), name="add_halves"
            )
            own, messages = Box(mine), [Box(over_high(message, step))]
            step *= 2
        return own, messages

    def sum_chunks(cs, own, messages):
        shape = (block, len(cs) * width)
        total = kernel_call(
            add_up,
            like(shape, F32),
            (ids, own.value.reshape(shape), *[m.value.reshape(shape) for m in messages]),
            name="add_up",
        )
        for i, c in enumerate(cs):
            sums[c] = total[:, i * width : (i + 1) * width]
        return Box(total)

    send_chunk(0)
    tie(amp, inter[0])
    send_chunk(1)
    tie(amp, inter[1], kept[2], all_kept)
    kept[3] = Box(over_col(kept[2].value, 1))
    all_kept = Box(place(kept, all_kept.value, False))
    tie(amp, all_kept)
    send_chunk(2)
    stage01 = keep_chunks((0, 1))
    tie(amp, stage01[0])
    send_chunk(3)
    tie(amp, inter[3], got[2])
    send_chunk(4)
    tie(inter[4], stage01[1][0], all_kept)
    stage01 = add_stages(*stage01)
    tie(stage01[0], all_kept)
    stage2 = keep_chunks((2,))
    tie(stage2[0], all_kept)
    stage3 = keep_chunks((3,))
    tie(stage3[0], stage2[1][0])
    stage2 = add_stages(*stage2)
    tie(stage2[0], stage01[1][0])
    total = sum_chunks((0, 1), *stage01)
    tie(stage2[0], all_kept)
    stage4 = keep_chunks((4,), direct=True)
    tie(stage4[0], stage3[1][0])
    stage3 = add_stages(*stage3)
    sum_chunks((2,), *stage2)
    sum_chunks((3,), *stage3)
    sum_chunks((4,), *stage4)
    parts = []
    for (piece, _, _), spans in zip(order, where, strict=True):
        part = jnp.concatenate([sums[c][:, s : s + n] for c, s, n in spans], axis=1)
        parts.append(over_col(part, piece) if piece else part)
    out = kernel_call(
        functools.partial(finish, order),
        like((n_pair, block, piece_rows), F32),
        (ids, *parts),
        scratch=[pltpu.VMEM((n_pair, block, piece_rows), F32), pltpu.SemaphoreType.DMA((n_pair,))],
        name="finish",
        out_spec=HBM,
    )
    return out.transpose(0, 2, 1)


def solution(mesh):
    placed = (
        P(None, ("row", "col"), None),
        P("row", "col", None),
        P("row", None, None),
        P(),
        P(),
        P(),
    )
    return jax.shard_map(
        functools.partial(local, mesh.shape["row"], mesh.shape["col"]),
        mesh=mesh,
        in_specs=placed,
        out_specs=P(None, "col", "row"),
        check_vma=False,
    )
```

```python
import functools

import jax
import jax.numpy as jnp
from jax import lax
from jax.experimental import pallas as pl
from jax.experimental.pallas import tpu as pltpu
from jax.sharding import PartitionSpec as P

TILE = 64
BF = jnp.bfloat16
F32 = jnp.float32
VMEM = pl.BlockSpec(memory_space=pltpu.VMEM)
SMEM = pl.BlockSpec(memory_space=pltpu.SMEM)
HBM = pl.BlockSpec(memory_space=pltpu.HBM)
LIMIT = 10 * 2**20
COL, LOW, HIGH, ROW = range(4)


def kernel_call(body, outs, ins, scratch=(), name=None, out_spec=VMEM, aliases=None):
    return pl.pallas_call(
        body,
        out_shape=outs,
        in_specs=[SMEM] + [VMEM] * (len(ins) - 1),
        out_specs=jax.tree.map(lambda _: out_spec, outs),
        scratch_shapes=scratch,
        compiler_params=pltpu.CompilerParams(vmem_limit_bytes=LIMIT),
        cost_estimate=pl.CostEstimate(flops=0, bytes_accessed=0, transcendentals=0),
        input_output_aliases=aliases or {},
        name=name,
    )(*ins)


def like(shape, dtype):
    return jax.ShapeDtypeStruct(shape, dtype)


class Box:
    def __init__(self, value):
        self.value = value


def tie(*boxes):
    values = lax.optimization_barrier(tuple(box.value for box in boxes))
    for box, value in zip(boxes, values, strict=True):
        box.value = value


def iota(shape, dim):
    return lax.broadcasted_iota(jnp.int32, shape, dim)


def spread(row_tiles, tiles, size):
    count = tiles.shape[0]
    picker = (row_tiles == iota((row_tiles.shape[0], count), 1)).astype(F32).astype(BF)
    wide = (iota((count, size), 1) // TILE == iota((count, size), 0)).astype(F32).astype(BF)
    rows = jnp.dot(picker, tiles.astype(F32).astype(BF), preferred_element_type=F32).astype(BF)
    return jnp.dot(rows, wide, preferred_element_type=F32).astype(BF)


def mask_slab(n_col, ks, ids, tiles, *refs):
    pieces, out = refs[:-1], refs[-1]
    rows, size = pieces[0].shape
    for k, piece in zip(ks, pieces, strict=True):
        owner = ids[COL] ^ k
        row_tiles = ((ids[ROW] * n_col + owner) * rows + iota((rows, 1), 0)) // TILE
        out[owner % 2] = piece[...] * spread(row_tiles, tiles[...], size)


def place_blocks(places, ids, *refs):
    for place, block in zip(places, refs, strict=False):
        refs[-1][place(ids)] = block[...]


def masked_block(ids, tiles, piece, group, half, groups, block, size):
    first = ((piece * groups + group) * 2 + half) * block
    return spread((first + iota((block, 1), 0)) // TILE, tiles[...], size)


def place_pieces(ks, ids, tiles, *refs):
    pieces, (other, kept) = refs[: len(ks)], refs[len(ks) :]
    for k, piece in zip(ks, pieces, strict=True):
        aux, groups, _, block, size = piece.shape
        owner = ids[COL] ^ k
        for half, out in ((1 - ids[LOW], other), (ids[LOW], kept)):
            for g in range(groups):
                mask = masked_block(ids, tiles, owner, g, half, groups, block, size)
                for q in range(aux):
                    out[q, owner * groups + g] = piece[q, g, half] * mask


def place_halves(ks, other_half, ids, tiles, *refs):
    pieces, out = refs[: len(ks)], refs[-1]
    half = 1 - ids[LOW] if other_half else ids[LOW]
    for k, piece in zip(ks, pieces, strict=True):
        aux, groups, block, size = piece.shape
        owner = ids[COL] ^ k
        for g in range(groups):
            mask = masked_block(ids, tiles, owner, g, half, groups, block, size)
            for q in range(aux):
                out[q, owner * groups + g] = piece[q, g] * mask


def multiply_rows(factors, inter, carried, first, width):
    value = jnp.dot(carried[...], first[...], preferred_element_type=F32)
    for q in range(factors.shape[0]):
        value += lax.dot_general(
            factors[q],
            inter[pl.ds(q * width, width), :],
            (((1,), (1,)), ((), ())),
            preferred_element_type=F32,
        )
    return value


def runs(segments, block):
    found, to = [], 0
    for piece, start, count in segments:
        end = start + count
        while start < end:
            group, half, at = start // (2 * block), start // block % 2, start % block
            n = min(block - at, end - start)
            found.append((piece, group, half, at, n, to))
            start, to = start + n, to + n
    return found


def pick_rows(segments, width, ids, other, kept, picked):
    aux, n_high, block, _ = other.shape
    groups = max(1, n_high // 4)
    for low in range(2):

        @pl.when(ids[LOW] == low)
        def _():
            for piece, group, half, at, n, to in runs(segments, block):
                source = kept if half == low else other
                for q in range(aux):
                    picked[q * width + to : q * width + to + n, :] = source[
                        q, (ids[COL] ^ piece) * groups + group, at : at + n, :
                    ]


def times_amplitudes(picked, amp, inter, more=None):
    size = amp.shape[1]
    step = 256 if size % 256 == 0 else size
    rows = inter.shape[0]
    for i in range(size // step):
        at = slice(i * step, (i + 1) * step)
        value = jnp.dot(picked[...], amp[:, at], preferred_element_type=F32)
        inter[:, at] = value[:rows].astype(BF)
        if more is not None:
            more[:, at] = value[rows:]


def first_send_part(segments, width, ids, *refs):
    others, kepts, amp, factors, second, first, inter, send, other, kept, picked, rows, turned = refs
    aux = factors.shape[0]
    block = send.shape[1]
    pick_rows(segments, width, ids, others, kepts, picked)
    picked[aux * width :, :] = second[...]

    @pl.when(ids[LOW] >= 0)
    def _():
        times_amplitudes(picked, amp, inter, rows)

    @pl.when(ids[LOW] >= 0)
    def _():
        u = rows[...]
        high = u.astype(BF).astype(F32)
        turned[...] = jnp.concatenate([high[:aux], (u - high)[:aux]], axis=0).T
        for h in range(send.shape[0]):
            for half, out in ((1 - ids[LOW], other), (ids[LOW], kept)):
                at = pl.ds(pl.multiple_of((2 * h + half) * block, 8), block)
                out[h * block : (h + 1) * block, :] = turned[at, :].astype(BF)

    @pl.when(ids[LOW] >= 0)
    def _():
        value = multiply_rows(factors, inter, other, first, width)
        for h in range(send.shape[0]):
            send[h] = value[h * block : (h + 1) * block, :].astype(BF)


def send_part(segments, width, ids, *refs):
    others, kepts, amp, factors, carried, first, inter, send, picked = refs
    block = send.shape[1]
    pick_rows(segments, width, ids, others, kepts, picked)

    @pl.when(ids[LOW] >= 0)
    def _():
        times_amplitudes(picked, amp, inter)

    @pl.when(ids[LOW] >= 0)
    def _():
        value = multiply_rows(factors, inter, carried, first, width)
        for h in range(send.shape[0]):
            send[h] = value[h * block : (h + 1) * block, :].astype(BF)


def keep_rows(widths, ids, factors, carried, *refs):
    count = len(widths)
    inter, first, got = refs[:count], refs[count : 2 * count], refs[2 * count : 3 * count]
    total = refs[-1]
    block = got[0].shape[1]

    def part(c, at, width):
        @pl.when(ids[LOW] >= 0)
        def _():
            value = multiply_rows(factors, inter[c], carried, first[c], width)
            for h in range(got[c].shape[0]):
                total[h, :, at : at + width] = value[h * block : (h + 1) * block, :] + got[c][h].astype(F32)

    for c, width in enumerate(widths):
        part(c, sum(widths[:c]), width)
    return refs[3 * count : -1], total


def keep_direct(widths, ids, *refs):
    (own, *messages), total = keep_rows(widths, ids, *refs)
    own[...] = total[ids[HIGH]]
    for k, message in enumerate(messages, 1):
        message[...] = total[ids[HIGH] ^ k].astype(BF)


def keep_halves(widths, ids, *refs):
    (mine, message), total = keep_rows(widths, ids, *refs)
    for i in range(mine.shape[0]):
        mine[i] = total[ids[HIGH] ^ (2 * i)]
        message[i] = total[ids[HIGH] ^ (2 * i + 1)].astype(BF)


def add_halves(ids, mine, got, kept, message):
    for i in range(kept.shape[0]):
        kept[i] = mine[2 * i] + got[2 * i].astype(F32)
        message[i] = (mine[2 * i + 1] + got[2 * i + 1].astype(F32)).astype(BF)


def add_up(ids, own, *refs):
    value = own[...]
    for got in refs[:-1]:
        value += got[...].astype(F32)
    refs[-1][...] = value


def finish(places, ids, *refs):
    parts, out, whole, sems = refs[:-3], refs[-3], refs[-2], refs[-1]
    copies = []
    for k in range(whole.shape[0]):
        for (piece, start, count), part in zip(places, parts, strict=True):
            if piece == k:
                whole[k, :, start : start + count] = part[...]
        copy = pltpu.make_async_copy(whole.at[k], out.at[ids[COL] ^ k], sems.at[k])
        copy.start()
        copies.append(copy)
    for copy in copies:
        copy.wait()


def local(n_row, n_col, amplitudes, integrals, occupied, pairs, amp_tiles, int_tiles):
    n_pair, chunk_rows, size = amplitudes.shape
    aux, piece_rows, _ = integrals.shape
    n_high = n_row // 2
    block = size // n_row
    groups = piece_rows // (2 * block)
    half_size = n_high * block
    col, row = lax.axis_index("col"), lax.axis_index("row")
    ids = jnp.stack([col, row % 2, row // 2, row]).astype(jnp.int32)

    def over_col(x, k):
        return lax.ppermute(x, "col", [(i, i ^ k) for i in range(n_col)])

    def over_low(x):
        return lax.ppermute(x, "row", [(i, i ^ 1) for i in range(n_row)])

    def over_high(x, k):
        return lax.ppermute(x, "row", [(i, (i // 2 ^ k) * 2 + i % 2) for i in range(n_row)])

    def up(x):
        return lax.ppermute(x, "row", [(i, (i + 2) % n_row) for i in range(n_row)])

    mine = [lax.dynamic_index_in_dim(amplitudes, col ^ k, 0, keepdims=False) for k in range(n_col)]
    mine = [Box(mine[0])] + [Box(over_col(mine[k], k)) for k in range(1, n_col)]
    split = integrals.reshape(aux, groups, 2, block, size)
    low = row % 2
    other, kept = {}, {}
    split1 = Box(over_col(integrals, 1))
    tie(split1, mine[1])
    split_other, split_kept = Box(split), Box(split)

    def half_rows(box, half):
        return Box(lax.dynamic_index_in_dim(box.value, half, 2, keepdims=False))

    is_col = jnp.arange(n_pair, dtype=jnp.int32) == col
    pair_tiles = Box(jnp.sum(jnp.where(is_col[:, None, None], amp_tiles, 0), axis=0))
    tie(pair_tiles, mine[1])

    pair = jnp.sum(jnp.where(is_col[:, None], pairs, 0), axis=0)
    orbitals = jnp.arange(occupied.shape[1], dtype=jnp.int32)
    picks = (pair[:, None] == orbitals[None, :]).astype(BF)
    rows = jnp.einsum("po,qov->pqv", picks, occupied, preferred_element_type=F32).astype(BF)
    first, second = rows[0], rows[1]
    second = jnp.concatenate([second, jnp.zeros((16 - aux, size), BF)], axis=0)
    first = first.reshape(aux, n_col, piece_rows)
    first = [lax.dynamic_index_in_dim(first, col ^ k, 1, keepdims=False) for k in range(n_col)]
    first = [jnp.concatenate([x, x], axis=0) for x in first]

    step = min(256, piece_rows)
    widths = [step, 2 * piece_rows - step, 2 * piece_rows - step, step]
    cut = max(piece_rows - widths[-1], 0)
    order = [(1, 0, piece_rows), (0, 0, piece_rows), (2, 0, piece_rows), (3, 0, cut), (3, cut, piece_rows - cut)]
    order = [part for part in order if part[2]]
    chunks, where = [[] for _ in widths], []
    at = 0
    for piece, start, count in order:
        spans = []
        while count:
            done = sum(n for _, _, n in chunks[at])
            n = min(count, widths[at] - done)
            chunks[at].append((piece, start, n))
            spans.append((at, done, n))
            start, count = start + n, count - n
            at += done + n == widths[at]
        where.append(spans)
    first = [jnp.concatenate([first[p][:, s : s + n] for p, s, n in chunk], axis=1) for chunk in chunks]

    second, first = Box(second), [Box(x) for x in first]

    def half_slab(ks):
        return kernel_call(
            functools.partial(mask_slab, n_col, ks),
            like((2, chunk_rows, size), BF),
            (ids, pair_tiles.value, *[mine[k].value for k in ks]),
            name="half_slab",
        ).reshape(2 * chunk_rows, size)

    shape = like((aux, n_high, block, size), BF)
    all_other, all_kept = map(
        Box,
        kernel_call(
            functools.partial(place_pieces, (0, 1)),
            (shape, shape),
            (ids, int_tiles, split, split1.value.reshape(split.shape)),
            name="place_pieces",
        ),
    )

    def place(pieces, k, into, other_half):
        return kernel_call(
            functools.partial(place_halves, (k,), other_half),
            shape,
            (ids, int_tiles, pieces[k].value, into.value),
            aliases={3: 0},
            name="place_halves",
        )

    def flat(x):
        return x.reshape(aux, half_size, size)

    def slab_place(step, other_low, side, ids):
        h = lax.rem(ids[HIGH] + (n_high - step), n_high)
        low = 1 - ids[LOW] if other_low else ids[LOW]
        return (h * 2 + low) * 2 + (ids[COL] // 2 ^ side)

    def place_slabs(found):
        places = [functools.partial(slab_place, *place) for _, place in found]
        return kernel_call(
            functools.partial(place_blocks, places),
            like((n_row * 2, 2 * chunk_rows, size), BF),
            (ids, *[slab.value for slab, _ in found]),
            name="place_rows",
        )

    rings = [[Box(half_slab((0, 1)))]]
    tie(split_other, rings[0][0])
    send_other = half_rows(split_other, 1 - low)
    other[2] = Box(over_col(send_other.value, 2))
    swapped = [[], []]

    def hop(r, s):
        ring = rings[r]
        if s > 0:
            tie(ring[s], swapped[r][-1])
        if s + 1 < n_high:
            ring.append(Box(up(ring[s].value)))
        swapped[r].append(Box(over_low(ring[s].value)))

    tie(rings[0][0], mine[2], mine[3])
    rings.append([Box(half_slab((2, 3)))])
    hop(0, 0)
    hop(1, 0)
    tie(rings[0][1], second, *first)
    tie(rings[0][1], split_kept)
    send_kept = half_rows(split_kept, low)
    tie(rings[0][1], send_kept)
    tie(rings[1][1], all_other, all_kept)
    for s in range(1, n_high):
        hop(0, s)
        hop(1, s)
    tie(other[2], rings[0][-1], rings[1][-1])
    other[3] = Box(over_col(other[2].value, 1))
    kept[2] = Box(over_col(send_kept.value, 2))
    all_other = Box(place(other, 2, all_other, True))
    found = [(slab, (s, low, r)) for low, side in enumerate((rings, swapped)) for r in range(2) for s, slab in enumerate(side[r])]
    amp = Box(place_slabs(found).reshape(size, size))
    all_other = Box(place(other, 3, all_other, True))

    inter, got, sums, carried = {}, {}, {}, []

    def send_chunk(c):
        pieces = (all_other.value, all_kept.value)
        width = widths[c]
        outs = (like((aux * width, size), BF), like((n_high, block, width), BF))
        if not carried:
            extra = second.value.shape[0]
            x, send, *terms = kernel_call(
                functools.partial(first_send_part, chunks[c], width),
                outs + (like((half_size, 2 * aux), BF),) * 2,
                (ids, *pieces, amp.value, flat(all_other.value), second.value, first[c].value),
                scratch=[
                    pltpu.VMEM((aux * width + extra, size), BF),
                    pltpu.VMEM((extra, size), F32),
                    pltpu.VMEM((size, 2 * aux), F32),
                ],
                name="send_part",
            )
            carried.extend(terms)
        else:
            x, send = kernel_call(
                functools.partial(send_part, chunks[c], width),
                outs,
                (ids, *pieces, amp.value, flat(all_other.value), carried[0], first[c].value),
                scratch=[pltpu.VMEM((aux * width, size), BF)],
                name="send_part",
            )
        inter[c] = Box(x)
        got[c] = Box(over_low(send))

    def keep_chunks(cs, direct=False):
        own_widths = tuple(widths[c] for c in cs)
        wide = sum(own_widths)
        half = n_high // 2
        if direct:
            body, outs = keep_direct, (like((block, wide), F32),) + (like((block, wide), BF),) * (n_high - 1)
        else:
            body, outs = keep_halves, (like((half, block, wide), F32), like((half, block, wide), BF))
        own, *messages = kernel_call(
            functools.partial(body, own_widths),
            outs,
            (ids, flat(all_kept.value), carried[1])
            + tuple(inter[c].value for c in cs)
            + tuple(first[c].value for c in cs)
            + tuple(got[c].value for c in cs),
            scratch=[pltpu.VMEM((n_high, block, wide), F32)],
            name="keep_part",
        )
        if direct:
            messages = [Box(over_high(m, k)) for k, m in enumerate(messages, 1)]
        else:
            messages = [Box(over_high(messages[0], 1))]
        return Box(own), messages

    def add_stages(own, messages):
        step = 2
        while own.value.shape[0] > 1:
            half = own.value.shape[0] // 2
            shape = (half,) + own.value.shape[1:]
            mine, message = kernel_call(
                add_halves, (like(shape, F32), like(shape, BF)), (ids, own.value, messages[0].value), name="add_halves"
            )
            own, messages = Box(mine), [Box(over_high(message, step))]
            step *= 2
        return own, messages

    def sum_chunks(cs, own, messages):
        shape = (block, sum(widths[c] for c in cs))
        total = kernel_call(
            add_up,
            like(shape, F32),
            (ids, own.value.reshape(shape), *[m.value.reshape(shape) for m in messages]),
            name="add_up",
        )
        total = Box(total)
        at = 0
        for c in cs:
            sums[c] = (total, at)
            at += widths[c]
        return total

    stages = {}
    last = amp

    def send_step(c):
        nonlocal last
        if c:
            tie(amp, last)
        send_chunk(c)
        last = inter[c]

    def place_step(k):
        nonlocal last, all_kept
        tie(all_kept, last)
        all_kept = Box(place(kept, k, all_kept, False))
        last = all_kept

    def keep_step(cs):
        nonlocal last
        tie(inter[cs[-1]], last)
        stages[cs] = keep_chunks(cs, direct=cs == (3,))
        last = stages[cs][0]

    def add_step(cs):
        nonlocal last
        tie(stages[cs][0], last)
        stages[cs] = add_stages(*stages[cs])
        last = stages[cs][0]

    def sum_step(cs):
        nonlocal last
        tie(stages[cs][0], last)
        last = sum_chunks(cs, *stages[cs])

    send_step(0)
    send_step(1)
    tie(last, got[0])
    tie(kept[2], last)
    kept[3] = Box(over_col(kept[2].value, 1))
    place_step(2)
    place_step(3)
    send_step(2)
    keep_step((0, 1))
    send_step(3)
    keep_step((2,))
    add_step((0, 1))
    add_step((2,))
    keep_step((3,))
    sum_step((0, 1))
    sum_step((2,))
    sum_step((3,))
    parts = []
    for (piece, _, _), spans in zip(order, where, strict=True):
        spans = [(sums[c][0].value, sums[c][1] + s, n) for c, s, n in spans]
        part = jnp.concatenate([total[:, s : s + n] for total, s, n in spans], axis=1)
        parts.append(over_col(part, piece) if piece else part)
    out = kernel_call(
        functools.partial(finish, order),
        like((n_pair, block, piece_rows), F32),
        (ids, *parts),
        scratch=[pltpu.VMEM((n_pair, block, piece_rows), F32), pltpu.SemaphoreType.DMA((n_pair,))],
        name="finish",
        out_spec=HBM,
    )
    return out.transpose(0, 2, 1)


def solution(mesh):
    placed = (
        P(None, ("row", "col"), None),
        P("row", "col", None),
        P("row", None, None),
        P(),
        P(),
        P(),
    )
    return jax.shard_map(
        functools.partial(local, mesh.shape["row"], mesh.shape["col"]),
        mesh=mesh,
        in_specs=placed,
        out_specs=P(None, "col", "row"),
        check_vma=False,
    )
```

```python
import functools

import jax
import jax.numpy as jnp
from jax import lax
from jax.experimental import pallas as pl
from jax.experimental.pallas import tpu as pltpu
from jax.sharding import PartitionSpec as P

TILE = 64
BF = jnp.bfloat16
F32 = jnp.float32
VMEM = pl.BlockSpec(memory_space=pltpu.VMEM)
SMEM = pl.BlockSpec(memory_space=pltpu.SMEM)
HBM = pl.BlockSpec(memory_space=pltpu.HBM)
LIMIT = 10 * 2**20
COL, LOW, HIGH, ROW = range(4)
ROWS_AT, PIECES_AT, KEPT_AT = (1, 0), (1, 1), (1, 0)
STEPS = (
    ("s", 0),
    ("s", 1),
    ("g", 0),
    ("f", 0),
    ("p", 2),
    ("p", 3),
    ("s", 2),
    ("k", (0, 1)),
    ("s", 3),
    ("k", (2,)),
    ("a", (0, 1)),
    ("a", (2,)),
    ("k", (3,)),
    ("u", (0, 1)),
    ("u", (2,)),
    ("u", (3,)),
)


def kernel_call(body, outs, ins, scratch=(), name=None, out_spec=VMEM, aliases=None):
    return pl.pallas_call(
        body,
        out_shape=outs,
        in_specs=[SMEM] + [VMEM] * (len(ins) - 1),
        out_specs=jax.tree.map(lambda _: out_spec, outs),
        scratch_shapes=scratch,
        compiler_params=pltpu.CompilerParams(vmem_limit_bytes=LIMIT),
        cost_estimate=pl.CostEstimate(flops=0, bytes_accessed=0, transcendentals=0),
        input_output_aliases=aliases or {},
        name=name,
    )(*ins)


def like(shape, dtype):
    return jax.ShapeDtypeStruct(shape, dtype)


class Box:
    def __init__(self, value):
        self.value = value


def tie(*boxes):
    values = lax.optimization_barrier(tuple(box.value for box in boxes))
    for box, value in zip(boxes, values, strict=True):
        box.value = value


def iota(shape, dim):
    return lax.broadcasted_iota(jnp.int32, shape, dim)


def spread(row_tiles, tiles, size):
    count = tiles.shape[0]
    picker = (row_tiles == iota((row_tiles.shape[0], count), 1)).astype(F32).astype(BF)
    wide = (iota((count, size), 1) // TILE == iota((count, size), 0)).astype(F32).astype(BF)
    rows = jnp.dot(picker, tiles.astype(F32).astype(BF), preferred_element_type=F32).astype(BF)
    return jnp.dot(rows, wide, preferred_element_type=F32).astype(BF)


def mask_slab(n_col, ks, ids, tiles, *refs):
    pieces, out = refs[:-1], refs[-1]
    rows, size = pieces[0].shape
    for k, piece in zip(ks, pieces, strict=True):
        owner = ids[COL] ^ k
        row_tiles = ((ids[ROW] * n_col + owner) * rows + iota((rows, 1), 0)) // TILE
        out[owner % 2] = piece[...] * spread(row_tiles, tiles[...], size)


def place_blocks(places, ids, *refs):
    for place, block in zip(places, refs, strict=False):
        refs[-1][place(ids)] = block[...]


def masked_block(ids, tiles, piece, group, half, groups, block, size):
    first = ((piece * groups + group) * 2 + half) * block
    return spread((first + iota((block, 1), 0)) // TILE, tiles[...], size)


def place_pieces(ks, ids, tiles, *refs):
    pieces, (other, kept) = refs[: len(ks)], refs[len(ks) :]
    for k, piece in zip(ks, pieces, strict=True):
        aux, groups, _, block, size = piece.shape
        owner = ids[COL] ^ k
        for half, out in ((1 - ids[LOW], other), (ids[LOW], kept)):
            for g in range(groups):
                mask = masked_block(ids, tiles, owner, g, half, groups, block, size)
                for q in range(aux):
                    out[q, owner * groups + g] = piece[q, g, half] * mask


def place_halves(ks, other_half, ids, tiles, *refs):
    pieces, out = refs[: len(ks)], refs[-1]
    half = 1 - ids[LOW] if other_half else ids[LOW]
    for k, piece in zip(ks, pieces, strict=True):
        aux, groups, block, size = piece.shape
        owner = ids[COL] ^ k
        for g in range(groups):
            mask = masked_block(ids, tiles, owner, g, half, groups, block, size)
            for q in range(aux):
                out[q, owner * groups + g] = piece[q, g] * mask


def multiply_rows(factors, inter, carried, first, width):
    value = jnp.dot(carried[...], first[...], preferred_element_type=F32)
    for q in range(factors.shape[0]):
        value += lax.dot_general(
            factors[q],
            inter[pl.ds(q * width, width), :],
            (((1,), (1,)), ((), ())),
            preferred_element_type=F32,
        )
    return value


def runs(segments, block):
    found, to = [], 0
    for piece, start, count in segments:
        end = start + count
        while start < end:
            group, half, at = start // (2 * block), start // block % 2, start % block
            n = min(block - at, end - start)
            found.append((piece, group, half, at, n, to))
            start, to = start + n, to + n
    return found


def pick_rows(segments, width, ids, other, kept, picked):
    aux, n_high, block, _ = other.shape
    groups = max(1, n_high // 4)
    for low in range(2):

        @pl.when(ids[LOW] == low)
        def _():
            for piece, group, half, at, n, to in runs(segments, block):
                source = kept if half == low else other
                for q in range(aux):
                    picked[q * width + to : q * width + to + n, :] = source[
                        q, (ids[COL] ^ piece) * groups + group, at : at + n, :
                    ]


def times_amplitudes(picked, amp, inter, more=None):
    size = amp.shape[1]
    step = 256 if size % 256 == 0 else size
    rows = inter.shape[0]
    for i in range(size // step):
        at = slice(i * step, (i + 1) * step)
        value = jnp.dot(picked[...], amp[:, at], preferred_element_type=F32)
        inter[:, at] = value[:rows].astype(BF)
        if more is not None:
            more[:, at] = value[rows:]


def first_send_part(segments, width, ids, *refs):
    others, kepts, amp, factors, second, first, inter, send, other, kept, picked, rows, turned = refs
    aux = factors.shape[0]
    block = send.shape[1]
    pick_rows(segments, width, ids, others, kepts, picked)
    picked[aux * width :, :] = second[...]

    @pl.when(ids[LOW] >= 0)
    def _():
        times_amplitudes(picked, amp, inter, rows)

    @pl.when(ids[LOW] >= 0)
    def _():
        u = rows[...]
        high = u.astype(BF).astype(F32)
        turned[...] = jnp.concatenate([high[:aux], (u - high)[:aux]], axis=0).T
        for h in range(send.shape[0]):
            for half, out in ((1 - ids[LOW], other), (ids[LOW], kept)):
                at = pl.ds(pl.multiple_of((2 * h + half) * block, 8), block)
                out[h * block : (h + 1) * block, :] = turned[at, :].astype(BF)

    @pl.when(ids[LOW] >= 0)
    def _():
        value = multiply_rows(factors, inter, other, first, width)
        for h in range(send.shape[0]):
            send[h] = value[h * block : (h + 1) * block, :].astype(BF)


def send_part(segments, width, ids, *refs):
    others, kepts, amp, factors, carried, first, inter, send, picked = refs
    block = send.shape[1]
    pick_rows(segments, width, ids, others, kepts, picked)

    @pl.when(ids[LOW] >= 0)
    def _():
        times_amplitudes(picked, amp, inter)

    @pl.when(ids[LOW] >= 0)
    def _():
        value = multiply_rows(factors, inter, carried, first, width)
        for h in range(send.shape[0]):
            send[h] = value[h * block : (h + 1) * block, :].astype(BF)


def keep_rows(widths, ids, factors, carried, *refs):
    count = len(widths)
    inter, first, got = refs[:count], refs[count : 2 * count], refs[2 * count : 3 * count]
    total = refs[-1]
    block = got[0].shape[1]

    def part(c, at, width):
        @pl.when(ids[LOW] >= 0)
        def _():
            value = multiply_rows(factors, inter[c], carried, first[c], width)
            for h in range(got[c].shape[0]):
                total[h, :, at : at + width] = value[h * block : (h + 1) * block, :] + got[c][h].astype(F32)

    for c, width in enumerate(widths):
        part(c, sum(widths[:c]), width)
    return refs[3 * count : -1], total


def keep_direct(widths, ids, *refs):
    (own, *messages), total = keep_rows(widths, ids, *refs)
    own[...] = total[ids[HIGH]]
    for k, message in enumerate(messages, 1):
        message[...] = total[ids[HIGH] ^ k].astype(BF)


def keep_halves(widths, ids, *refs):
    (mine, message), total = keep_rows(widths, ids, *refs)
    for i in range(mine.shape[0]):
        mine[i] = total[ids[HIGH] ^ (2 * i)]
        message[i] = total[ids[HIGH] ^ (2 * i + 1)].astype(BF)


def add_halves(ids, mine, got, kept, message):
    for i in range(kept.shape[0]):
        kept[i] = mine[2 * i] + got[2 * i].astype(F32)
        message[i] = (mine[2 * i + 1] + got[2 * i + 1].astype(F32)).astype(BF)


def add_up(ids, own, *refs):
    value = own[...]
    for got in refs[:-1]:
        value += got[...].astype(F32)
    refs[-1][...] = value


def finish(places, ids, *refs):
    parts, out, whole, sems = refs[:-3], refs[-3], refs[-2], refs[-1]
    copies = []
    for k in range(whole.shape[0]):
        for (piece, start, count), part in zip(places, parts, strict=True):
            if piece == k:
                whole[k, :, start : start + count] = part[:, :count]
        copy = pltpu.make_async_copy(whole.at[k], out.at[ids[COL] ^ k], sems.at[k])
        copy.start()
        copies.append(copy)
    for copy in copies:
        copy.wait()


def local(n_row, n_col, amplitudes, integrals, occupied, pairs, amp_tiles, int_tiles):
    n_pair, chunk_rows, size = amplitudes.shape
    aux, piece_rows, _ = integrals.shape
    n_high = n_row // 2
    block = size // n_row
    groups = piece_rows // (2 * block)
    half_size = n_high * block
    col, row = lax.axis_index("col"), lax.axis_index("row")
    ids = jnp.stack([col, row % 2, row // 2, row]).astype(jnp.int32)

    def over_col(x, k):
        return lax.ppermute(x, "col", [(i, i ^ k) for i in range(n_col)])

    def over_low(x):
        return lax.ppermute(x, "row", [(i, i ^ 1) for i in range(n_row)])

    def over_high(x, k):
        return lax.ppermute(x, "row", [(i, (i // 2 ^ k) * 2 + i % 2) for i in range(n_row)])

    def up(x):
        return lax.ppermute(x, "row", [(i, (i + 2) % n_row) for i in range(n_row)])

    mine = [lax.dynamic_index_in_dim(amplitudes, col ^ k, 0, keepdims=False) for k in range(n_col)]
    mine = [Box(mine[0])] + [Box(over_col(mine[k], k)) for k in range(1, n_col)]
    split = integrals.reshape(aux, groups, 2, block, size)
    low = row % 2
    other, kept = {}, {}
    split1 = Box(over_col(integrals, 1))
    tie(split1, mine[1])
    split_other, split_kept = Box(split), Box(split)

    def half_rows(box, half):
        return Box(lax.dynamic_index_in_dim(box.value, half, 2, keepdims=False))

    is_col = jnp.arange(n_pair, dtype=jnp.int32) == col
    pair_tiles = Box(jnp.sum(jnp.where(is_col[:, None, None], amp_tiles, 0), axis=0))
    tie(pair_tiles, mine[1])

    pair = jnp.sum(jnp.where(is_col[:, None], pairs, 0), axis=0)
    orbitals = jnp.arange(occupied.shape[1], dtype=jnp.int32)
    picks = (pair[:, None] == orbitals[None, :]).astype(BF)
    rows = jnp.einsum("po,qov->pqv", picks, occupied, preferred_element_type=F32).astype(BF)
    first, second = rows[0], rows[1]
    second = jnp.concatenate([second, jnp.zeros((16 - aux, size), BF)], axis=0)
    first = first.reshape(aux, n_col, piece_rows)
    first = [lax.dynamic_index_in_dim(first, col ^ k, 1, keepdims=False) for k in range(n_col)]
    first = [jnp.concatenate([x, x], axis=0) for x in first]

    step = min(256, piece_rows)
    widths = [step, 2 * piece_rows - step, 2 * piece_rows - step, step]
    cut = max(piece_rows - widths[-1], 0)
    order = [(1, 0, piece_rows), (0, 0, piece_rows), (2, 0, piece_rows), (3, 0, cut), (3, cut, piece_rows - cut)]
    order = [part for part in order if part[2]]
    chunks, where = [[] for _ in widths], []
    at = 0
    for piece, start, count in order:
        spans = []
        while count:
            done = sum(n for _, _, n in chunks[at])
            n = min(count, widths[at] - done)
            chunks[at].append((piece, start, n))
            spans.append((at, done, n))
            start, count = start + n, count - n
            at += done + n == widths[at]
        where.append(spans)
    first = [jnp.concatenate([first[p][:, s : s + n] for p, s, n in chunk], axis=1) for chunk in chunks]

    second, first = Box(second), [Box(x) for x in first]

    def half_slab(ks):
        return kernel_call(
            functools.partial(mask_slab, n_col, ks),
            like((2, chunk_rows, size), BF),
            (ids, pair_tiles.value, *[mine[k].value for k in ks]),
            name="half_slab",
        ).reshape(2 * chunk_rows, size)

    shape = like((aux, n_high, block, size), BF)
    all_other, all_kept = map(
        Box,
        kernel_call(
            functools.partial(place_pieces, (0, 1)),
            (shape, shape),
            (ids, int_tiles, split, split1.value.reshape(split.shape)),
            name="place_pieces",
        ),
    )

    def place(pieces, k, into, other_half):
        return kernel_call(
            functools.partial(place_halves, (k,), other_half),
            shape,
            (ids, int_tiles, pieces[k].value, into.value),
            aliases={3: 0},
            name="place_halves",
        )

    def flat(x):
        return x.reshape(aux, half_size, size)

    def slab_place(step, other_low, side, ids):
        h = lax.rem(ids[HIGH] + (n_high - step), n_high)
        low = 1 - ids[LOW] if other_low else ids[LOW]
        return (h * 2 + low) * 2 + (ids[COL] // 2 ^ side)

    def place_slabs(found):
        places = [functools.partial(slab_place, *place) for _, place in found]
        return kernel_call(
            functools.partial(place_blocks, places),
            like((n_row * 2, 2 * chunk_rows, size), BF),
            (ids, *[slab.value for slab, _ in found]),
            name="place_rows",
        )

    rings = [[Box(half_slab((0, 1)))]]
    tie(split_other, rings[0][0])
    send_other = half_rows(split_other, 1 - low)
    other[2] = Box(over_col(send_other.value, 2))
    swapped = [[], []]

    def hop(r, s):
        nonlocal send_kept
        ring = rings[r]
        if s > 0 and not (s == n_high - 1 and r == 1):
            tie(ring[s], swapped[r][-1])
        if (s, r) == ROWS_AT:
            tie(ring[s], second, *first)
        if (s, r) == PIECES_AT:
            tie(ring[s], all_other, all_kept)
        if (s, r) == KEPT_AT:
            tie(ring[s], split_kept)
            send_kept = half_rows(split_kept, low)
            tie(ring[s], send_kept)
        if s + 1 < n_high:
            ring.append(Box(up(ring[s].value)))
        if s == n_high - 1 and r == 1:
            swapped[r].append(Box(up(swapped[r][-1].value)))
        else:
            swapped[r].append(Box(over_low(ring[s].value)))

    send_kept = None
    tie(rings[0][0], mine[2], mine[3])
    rings.append([Box(half_slab((2, 3)))])
    for s in range(n_high):
        hop(0, s)
        hop(1, s)
    tie(other[2], rings[0][-1], rings[1][-1], swapped[1][-2])
    other[3] = Box(over_col(other[2].value, 1))
    kept[2] = Box(over_col(send_kept.value, 2))
    all_other = Box(place(other, 2, all_other, True))
    found = [(slab, (s, low, r)) for low, side in enumerate((rings, swapped)) for r in range(2) for s, slab in enumerate(side[r])]
    amp = Box(place_slabs(found).reshape(size, size))
    all_other = Box(place(other, 3, all_other, True))

    inter, got, sums, carried = {}, {}, {}, []

    def send_chunk(c):
        pieces = (all_other.value, all_kept.value)
        width = widths[c]
        outs = (like((aux * width, size), BF), like((n_high, block, width), BF))
        if not carried:
            extra = second.value.shape[0]
            x, send, *terms = kernel_call(
                functools.partial(first_send_part, chunks[c], width),
                outs + (like((half_size, 2 * aux), BF),) * 2,
                (ids, *pieces, amp.value, flat(all_other.value), second.value, first[c].value),
                scratch=[
                    pltpu.VMEM((aux * width + extra, size), BF),
                    pltpu.VMEM((extra, size), F32),
                    pltpu.VMEM((size, 2 * aux), F32),
                ],
                name="send_part",
            )
            carried.extend(terms)
        else:
            x, send = kernel_call(
                functools.partial(send_part, chunks[c], width),
                outs,
                (ids, *pieces, amp.value, flat(all_other.value), carried[0], first[c].value),
                scratch=[pltpu.VMEM((aux * width, size), BF)],
                name="send_part",
            )
        inter[c] = Box(x)
        send = Box(send)
        tie(send)
        got[c] = Box(over_low(send.value))

    def keep_chunks(cs, direct=False):
        own_widths = tuple(widths[c] for c in cs)
        wide = sum(own_widths)
        half = n_high // 2
        if direct:
            body, outs = keep_direct, (like((block, wide), F32),) + (like((block, wide), BF),) * (n_high - 1)
        else:
            body, outs = keep_halves, (like((half, block, wide), F32), like((half, block, wide), BF))
        own, *messages = kernel_call(
            functools.partial(body, own_widths),
            outs,
            (ids, flat(all_kept.value), carried[1])
            + tuple(inter[c].value for c in cs)
            + tuple(first[c].value for c in cs)
            + tuple(got[c].value for c in cs),
            scratch=[pltpu.VMEM((n_high, block, wide), F32)],
            name="keep_part",
        )
        if direct:
            messages = [Box(over_high(m, k)) for k, m in enumerate(messages, 1)]
        else:
            messages = [Box(over_high(messages[0], 1))]
        return Box(own), messages

    def add_stages(own, messages):
        step = 2
        while own.value.shape[0] > 1:
            half = own.value.shape[0] // 2
            shape = (half,) + own.value.shape[1:]
            mine, message = kernel_call(
                add_halves, (like(shape, F32), like(shape, BF)), (ids, own.value, messages[0].value), name="add_halves"
            )
            own, messages = Box(mine), [Box(over_high(message, step))]
            step *= 2
        return own, messages

    def sum_chunks(cs, own, messages):
        shape = (block, sum(widths[c] for c in cs))
        total = kernel_call(
            add_up,
            like(shape, F32),
            (ids, own.value.reshape(shape), *[m.value.reshape(shape) for m in messages]),
            name="add_up",
        )
        total = Box(total)
        at = 0
        for c in cs:
            sums[c] = (total, at)
            at += widths[c]
        return total

    stages = {}
    last = amp

    def send_step(c):
        nonlocal last
        if c:
            tie(amp, last)
        send_chunk(c)
        last = inter[c]

    def place_step(k):
        nonlocal last, all_kept
        tie(all_kept, last)
        all_kept = Box(place(kept, k, all_kept, False))
        last = all_kept

    def keep_step(cs):
        nonlocal last
        tie(inter[cs[-1]], last)
        stages[cs] = keep_chunks(cs, direct=cs == (3,))
        last = stages[cs][0]

    def add_step(cs):
        nonlocal last
        tie(stages[cs][0], last)
        stages[cs] = add_stages(*stages[cs])
        last = stages[cs][0]

    def sum_step(cs):
        nonlocal last
        tie(stages[cs][0], last)
        last = sum_chunks(cs, *stages[cs])

    def got_step(c):
        nonlocal last
        tie(last, got[c])

    def forward_step(c):
        tie(kept[2], last)
        kept[3] = Box(over_col(kept[2].value, 1))

    steps = {
        "s": send_step,
        "p": place_step,
        "k": keep_step,
        "a": add_step,
        "u": sum_step,
        "g": got_step,
        "f": forward_step,
    }
    for kind, what in STEPS:
        steps[kind](what)
    parts, places = [], []
    for (piece, start, count), spans in zip(order, where, strict=True):
        if spans[0][0] == 2 and piece == 3:
            part = over_col(parts[-1][:, widths[2] - count :], 1)
        elif spans[0][0] == 2:
            part = over_col(sums[2][0].value, piece)
        else:
            spans = [(sums[c][0].value, sums[c][1] + s, n) for c, s, n in spans]
            part = jnp.concatenate([total[:, s : s + n] for total, s, n in spans], axis=1)
            part = over_col(part, piece) if piece else part
        parts.append(part)
        places.append((piece, start, count))
    out = kernel_call(
        functools.partial(finish, places),
        like((n_pair, block, piece_rows), F32),
        (ids, *parts),
        scratch=[pltpu.VMEM((n_pair, block, piece_rows), F32), pltpu.SemaphoreType.DMA((n_pair,))],
        name="finish",
        out_spec=HBM,
    )
    return out.transpose(0, 2, 1)


def solution(mesh):
    placed = (
        P(None, ("row", "col"), None),
        P("row", "col", None),
        P("row", None, None),
        P(),
        P(),
        P(),
    )
    return jax.shard_map(
        functools.partial(local, mesh.shape["row"], mesh.shape["col"]),
        mesh=mesh,
        in_specs=placed,
        out_specs=P(None, "col", "row"),
        check_vma=False,
    )
```

```python
import functools

import jax
import jax.numpy as jnp
from jax import lax
from jax.experimental import pallas as pl
from jax.experimental.pallas import tpu as pltpu
from jax.sharding import PartitionSpec as P

TILE = 64
BF = jnp.bfloat16
F32 = jnp.float32
VMEM = pl.BlockSpec(memory_space=pltpu.VMEM)
SMEM = pl.BlockSpec(memory_space=pltpu.SMEM)
HBM = pl.BlockSpec(memory_space=pltpu.HBM)
LIMIT = 10 * 2**20
COL, LOW, HIGH, ROW = range(4)
ROWS_AT, PIECES_AT, KEPT_AT = (1, 0), (1, 1), (1, 0)
STEPS = (
    ("s", 0),
    ("s", 1),
    ("g", 0),
    ("f", 0),
    ("p", 2),
    ("p", 3),
    ("s", 2),
    ("k", (0, 1)),
    ("s", 3),
    ("k", (2,)),
    ("a", (0, 1)),
    ("a", (2,)),
    ("k", (3,)),
    ("u", (0, 1)),
    ("u", (2,)),
    ("u", (3,)),
)


def kernel_call(body, outs, ins, scratch=(), name=None, out_spec=VMEM, aliases=None):
    return pl.pallas_call(
        body,
        out_shape=outs,
        in_specs=[SMEM] + [VMEM] * (len(ins) - 1),
        out_specs=jax.tree.map(lambda _: out_spec, outs),
        scratch_shapes=scratch,
        compiler_params=pltpu.CompilerParams(vmem_limit_bytes=LIMIT),
        cost_estimate=pl.CostEstimate(flops=0, bytes_accessed=0, transcendentals=0),
        input_output_aliases=aliases or {},
        name=name,
    )(*ins)


def like(shape, dtype):
    return jax.ShapeDtypeStruct(shape, dtype)


class Box:
    def __init__(self, value):
        self.value = value


def tie(*boxes):
    values = lax.optimization_barrier(tuple(box.value for box in boxes))
    for box, value in zip(boxes, values, strict=True):
        box.value = value


def iota(shape, dim):
    return lax.broadcasted_iota(jnp.int32, shape, dim)


def spread(row_tiles, tiles, size):
    count = tiles.shape[0]
    picker = (row_tiles == iota((row_tiles.shape[0], count), 1)).astype(F32).astype(BF)
    wide = (iota((count, size), 1) // TILE == iota((count, size), 0)).astype(F32).astype(BF)
    rows = jnp.dot(picker, tiles.astype(F32).astype(BF), preferred_element_type=F32).astype(BF)
    return jnp.dot(rows, wide, preferred_element_type=F32).astype(BF)


def mask_slab(n_col, ks, ids, tiles, *refs):
    pieces, out = refs[:-1], refs[-1]
    rows, size = pieces[0].shape
    for k, piece in zip(ks, pieces, strict=True):
        owner = ids[COL] ^ k
        row_tiles = ((ids[ROW] * n_col + owner) * rows + iota((rows, 1), 0)) // TILE
        out[owner % 2] = piece[...] * spread(row_tiles, tiles[...], size)


def place_blocks(places, ids, *refs):
    for place, block in zip(places, refs, strict=False):
        refs[-1][place(ids)] = block[...]


def masked_block(ids, tiles, piece, group, half, groups, block, size):
    first = ((piece * groups + group) * 2 + half) * block
    return spread((first + iota((block, 1), 0)) // TILE, tiles[...], size)


def place_pieces(ks, ids, tiles, *refs):
    pieces, (other, kept) = refs[: len(ks)], refs[len(ks) :]
    for k, piece in zip(ks, pieces, strict=True):
        aux, groups, _, block, size = piece.shape
        owner = ids[COL] ^ k
        for half, out in ((1 - ids[LOW], other), (ids[LOW], kept)):
            for g in range(groups):
                mask = masked_block(ids, tiles, owner, g, half, groups, block, size)
                for q in range(aux):
                    out[q, owner * groups + g] = piece[q, g, half] * mask


def place_halves(ks, other_half, ids, tiles, *refs):
    pieces, out = refs[: len(ks)], refs[-1]
    half = 1 - ids[LOW] if other_half else ids[LOW]
    for k, piece in zip(ks, pieces, strict=True):
        aux, groups, block, size = piece.shape
        owner = ids[COL] ^ k
        for g in range(groups):
            mask = masked_block(ids, tiles, owner, g, half, groups, block, size)
            for q in range(aux):
                out[q, owner * groups + g] = piece[q, g] * mask


def place_parts(k, ids, tiles, *refs):
    out = refs[-1]
    pieces = refs[: out.shape[0]]
    owner = ids[COL] ^ k
    _, groups, block, size = pieces[0].shape
    for g in range(groups):
        mask = masked_block(ids, tiles, owner, g, 1 - ids[LOW], groups, block, size)
        for q, piece in enumerate(pieces):
            out[q, owner * groups + g] = piece[0, g] * mask


def multiply_rows(factors, inter, carried, first, width):
    value = jnp.dot(carried[...], first[...], preferred_element_type=F32)
    for q in range(factors.shape[0]):
        value += lax.dot_general(
            factors[q],
            inter[pl.ds(q * width, width), :],
            (((1,), (1,)), ((), ())),
            preferred_element_type=F32,
        )
    return value


def runs(segments, block):
    found, to = [], 0
    for piece, start, count in segments:
        end = start + count
        while start < end:
            group, half, at = start // (2 * block), start // block % 2, start % block
            n = min(block - at, end - start)
            found.append((piece, group, half, at, n, to))
            start, to = start + n, to + n
    return found


def pick_rows(segments, width, ids, other, kept, picked):
    aux, n_high, block, _ = other.shape
    groups = max(1, n_high // 4)
    for low in range(2):

        @pl.when(ids[LOW] == low)
        def _():
            for piece, group, half, at, n, to in runs(segments, block):
                source = kept if half == low else other
                for q in range(aux):
                    picked[q * width + to : q * width + to + n, :] = source[
                        q, (ids[COL] ^ piece) * groups + group, at : at + n, :
                    ]


def times_amplitudes(picked, amp, inter, more=None):
    size = amp.shape[1]
    step = 256 if size % 256 == 0 else size
    rows = inter.shape[0]
    for i in range(size // step):
        at = slice(i * step, (i + 1) * step)
        value = jnp.dot(picked[...], amp[:, at], preferred_element_type=F32)
        inter[:, at] = value[:rows].astype(BF)
        if more is not None:
            more[:, at] = value[rows:]


def first_send_part(segments, width, ids, *refs):
    others, kepts, amp, factors, second, first, inter, send, other, kept, picked, rows, turned = refs
    aux = factors.shape[0]
    block = send.shape[1]
    pick_rows(segments, width, ids, others, kepts, picked)
    picked[aux * width :, :] = second[...]

    @pl.when(ids[LOW] >= 0)
    def _():
        times_amplitudes(picked, amp, inter, rows)

    @pl.when(ids[LOW] >= 0)
    def _():
        u = rows[...]
        high = u.astype(BF).astype(F32)
        turned[...] = jnp.concatenate([high[:aux], (u - high)[:aux]], axis=0).T
        for h in range(send.shape[0]):
            for half, out in ((1 - ids[LOW], other), (ids[LOW], kept)):
                at = pl.ds(pl.multiple_of((2 * h + half) * block, 8), block)
                out[h * block : (h + 1) * block, :] = turned[at, :].astype(BF)

    @pl.when(ids[LOW] >= 0)
    def _():
        value = multiply_rows(factors, inter, other, first, width)
        for h in range(send.shape[0]):
            send[h] = value[h * block : (h + 1) * block, :].astype(BF)


def send_part(segments, width, ids, *refs):
    others, kepts, amp, factors, carried, first, inter, send, picked = refs
    block = send.shape[1]
    pick_rows(segments, width, ids, others, kepts, picked)

    @pl.when(ids[LOW] >= 0)
    def _():
        times_amplitudes(picked, amp, inter)

    @pl.when(ids[LOW] >= 0)
    def _():
        value = multiply_rows(factors, inter, carried, first, width)
        for h in range(send.shape[0]):
            send[h] = value[h * block : (h + 1) * block, :].astype(BF)


def keep_rows(widths, ids, factors, carried, *refs):
    count = len(widths)
    inter, first, got = refs[:count], refs[count : 2 * count], refs[2 * count : 3 * count]
    total = refs[-1]
    block = got[0].shape[1]

    def part(c, at, width):
        @pl.when(ids[LOW] >= 0)
        def _():
            value = multiply_rows(factors, inter[c], carried, first[c], width)
            for h in range(got[c].shape[0]):
                total[h, :, at : at + width] = value[h * block : (h + 1) * block, :] + got[c][h].astype(F32)

    for c, width in enumerate(widths):
        part(c, sum(widths[:c]), width)
    return refs[3 * count : -1], total


def keep_direct(widths, ids, *refs):
    (own, *messages), total = keep_rows(widths, ids, *refs)
    own[...] = total[ids[HIGH]]
    for k, message in enumerate(messages, 1):
        message[...] = total[ids[HIGH] ^ k].astype(BF)


def keep_halves(widths, ids, *refs):
    (mine, message), total = keep_rows(widths, ids, *refs)
    for i in range(mine.shape[0]):
        mine[i] = total[ids[HIGH] ^ (2 * i)]
        message[i] = total[ids[HIGH] ^ (2 * i + 1)].astype(BF)


def add_halves(ids, mine, got, kept, message):
    for i in range(kept.shape[0]):
        kept[i] = mine[2 * i] + got[2 * i].astype(F32)
        message[i] = (mine[2 * i + 1] + got[2 * i + 1].astype(F32)).astype(BF)


def add_up(ids, own, *refs):
    value = own[...]
    for got in refs[:-1]:
        value += got[...].astype(F32)
    refs[-1][...] = value


def finish(places, ids, *refs):
    parts, out, whole, sems = refs[:-3], refs[-3], refs[-2], refs[-1]
    copies = []
    for k in range(whole.shape[0]):
        for (piece, start, count), part in zip(places, parts, strict=True):
            if piece == k:
                whole[k, :, start : start + count] = part[:, :count]
        copy = pltpu.make_async_copy(whole.at[k], out.at[ids[COL] ^ k], sems.at[k])
        copy.start()
        copies.append(copy)
    for copy in copies:
        copy.wait()


def local(n_row, n_col, amplitudes, integrals, occupied, pairs, amp_tiles, int_tiles):
    n_pair, chunk_rows, size = amplitudes.shape
    aux, piece_rows, _ = integrals.shape
    n_high = n_row // 2
    block = size // n_row
    groups = piece_rows // (2 * block)
    half_size = n_high * block
    col, row = lax.axis_index("col"), lax.axis_index("row")
    ids = jnp.stack([col, row % 2, row // 2, row]).astype(jnp.int32)

    def over_col(x, k):
        return lax.ppermute(x, "col", [(i, i ^ k) for i in range(n_col)])

    def over_low(x):
        return lax.ppermute(x, "row", [(i, i ^ 1) for i in range(n_row)])

    def over_high(x, k):
        return lax.ppermute(x, "row", [(i, (i // 2 ^ k) * 2 + i % 2) for i in range(n_row)])

    def up(x):
        return lax.ppermute(x, "row", [(i, (i + 2) % n_row) for i in range(n_row)])

    mine = [lax.dynamic_index_in_dim(amplitudes, col ^ k, 0, keepdims=False) for k in range(n_col)]
    mine = [Box(mine[0])] + [Box(over_col(mine[k], k)) for k in range(1, n_col)]
    split = integrals.reshape(aux, groups, 2, block, size)
    low = row % 2
    other, kept = {}, {}
    split1 = Box(over_col(integrals, 1))
    tie(split1, mine[1])
    split_other, split_kept = Box(split), Box(split)

    def half_rows(box, half):
        return Box(lax.dynamic_index_in_dim(box.value, half, 2, keepdims=False))

    is_col = jnp.arange(n_pair, dtype=jnp.int32) == col
    pair_tiles = Box(jnp.sum(jnp.where(is_col[:, None, None], amp_tiles, 0), axis=0))
    tie(pair_tiles, mine[1])

    pair = jnp.sum(jnp.where(is_col[:, None], pairs, 0), axis=0)
    orbitals = jnp.arange(occupied.shape[1], dtype=jnp.int32)
    picks = (pair[:, None] == orbitals[None, :]).astype(BF)
    rows = jnp.einsum("po,qov->pqv", picks, occupied, preferred_element_type=F32).astype(BF)
    first, second = rows[0], rows[1]
    second = jnp.concatenate([second, jnp.zeros((16 - aux, size), BF)], axis=0)
    first = first.reshape(aux, n_col, piece_rows)
    first = [lax.dynamic_index_in_dim(first, col ^ k, 1, keepdims=False) for k in range(n_col)]
    first = [jnp.concatenate([x, x], axis=0) for x in first]

    step = min(256, piece_rows)
    widths = [step, 2 * piece_rows - step, 2 * piece_rows - step, step]
    cut = max(piece_rows - widths[-1], 0)
    order = [(1, 0, piece_rows), (0, 0, piece_rows), (2, 0, piece_rows), (3, 0, cut), (3, cut, piece_rows - cut)]
    order = [part for part in order if part[2]]
    chunks, where = [[] for _ in widths], []
    at = 0
    for piece, start, count in order:
        spans = []
        while count:
            done = sum(n for _, _, n in chunks[at])
            n = min(count, widths[at] - done)
            chunks[at].append((piece, start, n))
            spans.append((at, done, n))
            start, count = start + n, count - n
            at += done + n == widths[at]
        where.append(spans)
    first = [jnp.concatenate([first[p][:, s : s + n] for p, s, n in chunk], axis=1) for chunk in chunks]

    second, first = Box(second), [Box(x) for x in first]

    def half_slab(ks):
        return kernel_call(
            functools.partial(mask_slab, n_col, ks),
            like((2, chunk_rows, size), BF),
            (ids, pair_tiles.value, *[mine[k].value for k in ks]),
            name="half_slab",
        ).reshape(2 * chunk_rows, size)

    shape = like((aux, n_high, block, size), BF)
    all_other, all_kept = map(
        Box,
        kernel_call(
            functools.partial(place_pieces, (0, 1)),
            (shape, shape),
            (ids, int_tiles, split, split1.value.reshape(split.shape)),
            name="place_pieces",
        ),
    )

    def place(pieces, k, into, other_half):
        return kernel_call(
            functools.partial(place_halves, (k,), other_half),
            shape,
            (ids, int_tiles, pieces[k].value, into.value),
            aliases={3: 0},
            name="place_halves",
        )

    def flat(x):
        return x.reshape(aux, half_size, size)

    def slab_place(step, other_low, side, ids):
        h = lax.rem(ids[HIGH] + (n_high - step), n_high)
        low = 1 - ids[LOW] if other_low else ids[LOW]
        return (h * 2 + low) * 2 + (ids[COL] // 2 ^ side)

    def place_slabs(found):
        places = [functools.partial(slab_place, *place) for _, place in found]
        return kernel_call(
            functools.partial(place_blocks, places),
            like((n_row * 2, 2 * chunk_rows, size), BF),
            (ids, *[slab.value for slab, _ in found]),
            name="place_rows",
        )

    rings = [[Box(half_slab((0, 1)))]]
    tie(split_other, rings[0][0])
    send_other = half_rows(split_other, 1 - low)
    other[2] = Box(over_col(send_other.value, 2))
    swapped = [[], []]

    def hop(r, s):
        nonlocal send_kept
        ring = rings[r]
        if s > 0 and not (s == n_high - 1 and r == 1):
            tie(ring[s], swapped[r][-1])
        if (s, r) == ROWS_AT:
            tie(ring[s], second, *first)
        if (s, r) == PIECES_AT:
            tie(ring[s], all_other, all_kept)
        if (s, r) == KEPT_AT:
            tie(ring[s], split_kept)
            send_kept = half_rows(split_kept, low)
            tie(ring[s], send_kept)
        if s + 1 < n_high:
            ring.append(Box(up(ring[s].value)))
        if s == n_high - 1 and r == 1:
            swapped[r].append(Box(up(swapped[r][-1].value)))
        else:
            swapped[r].append(Box(over_low(ring[s].value)))

    send_kept = None
    tie(rings[0][0], mine[2], mine[3])
    rings.append([Box(half_slab((2, 3)))])
    for s in range(n_high):
        hop(0, s)
        hop(1, s)
    tie(other[2], rings[0][-1], rings[1][-1], swapped[1][-2])
    other[3] = [over_col(other[2].value[q : q + 1], 1) for q in range(aux)]
    kept[2] = Box(over_col(send_kept.value, 2))
    all_other = Box(place(other, 2, all_other, True))
    found = [(slab, (s, low, r)) for low, side in enumerate((rings, swapped)) for r in range(2) for s, slab in enumerate(side[r])]
    amp = Box(place_slabs(found).reshape(size, size))
    all_other = Box(
        kernel_call(
            functools.partial(place_parts, 3),
            shape,
            (ids, int_tiles, *other[3], all_other.value),
            aliases={2 + aux: 0},
            name="place_parts",
        )
    )

    inter, got, sums, carried = {}, {}, {}, []

    def send_chunk(c):
        pieces = (all_other.value, all_kept.value)
        width = widths[c]
        outs = (like((aux * width, size), BF), like((n_high, block, width), BF))
        if not carried:
            extra = second.value.shape[0]
            x, send, *terms = kernel_call(
                functools.partial(first_send_part, chunks[c], width),
                outs + (like((half_size, 2 * aux), BF),) * 2,
                (ids, *pieces, amp.value, flat(all_other.value), second.value, first[c].value),
                scratch=[
                    pltpu.VMEM((aux * width + extra, size), BF),
                    pltpu.VMEM((extra, size), F32),
                    pltpu.VMEM((size, 2 * aux), F32),
                ],
                name="send_part",
            )
            carried.extend(terms)
        else:
            x, send = kernel_call(
                functools.partial(send_part, chunks[c], width),
                outs,
                (ids, *pieces, amp.value, flat(all_other.value), carried[0], first[c].value),
                scratch=[pltpu.VMEM((aux * width, size), BF)],
                name="send_part",
            )
        inter[c] = Box(x)
        send = Box(send)
        tie(send)
        got[c] = Box(over_low(send.value))

    def keep_chunks(cs, direct=False):
        own_widths = tuple(widths[c] for c in cs)
        wide = sum(own_widths)
        half = n_high // 2
        if direct:
            body, outs = keep_direct, (like((block, wide), F32),) + (like((block, wide), BF),) * (n_high - 1)
        else:
            body, outs = keep_halves, (like((half, block, wide), F32), like((half, block, wide), BF))
        own, *messages = kernel_call(
            functools.partial(body, own_widths),
            outs,
            (ids, flat(all_kept.value), carried[1])
            + tuple(inter[c].value for c in cs)
            + tuple(first[c].value for c in cs)
            + tuple(got[c].value for c in cs),
            scratch=[pltpu.VMEM((n_high, block, wide), F32)],
            name="keep_part",
        )
        if direct:
            messages = [Box(over_high(m, k)) for k, m in enumerate(messages, 1)]
        else:
            messages = [Box(over_high(messages[0], 1))]
        return Box(own), messages

    def add_stages(own, messages):
        step = 2
        while own.value.shape[0] > 1:
            half = own.value.shape[0] // 2
            shape = (half,) + own.value.shape[1:]
            mine, message = kernel_call(
                add_halves, (like(shape, F32), like(shape, BF)), (ids, own.value, messages[0].value), name="add_halves"
            )
            own, messages = Box(mine), [Box(over_high(message, step))]
            step *= 2
        return own, messages

    def sum_chunks(cs, own, messages):
        shape = (block, sum(widths[c] for c in cs))
        total = kernel_call(
            add_up,
            like(shape, F32),
            (ids, own.value.reshape(shape), *[m.value.reshape(shape) for m in messages]),
            name="add_up",
        )
        total = Box(total)
        at = 0
        for c in cs:
            sums[c] = (total, at)
            at += widths[c]
        return total

    stages = {}
    last = amp

    def send_step(c):
        nonlocal last
        if c:
            tie(amp, last)
        send_chunk(c)
        last = inter[c]

    def place_step(k):
        nonlocal last, all_kept
        tie(all_kept, last)
        all_kept = Box(place(kept, k, all_kept, False))
        last = all_kept

    def keep_step(cs):
        nonlocal last
        tie(inter[cs[-1]], last)
        stages[cs] = keep_chunks(cs, direct=cs == (3,))
        last = stages[cs][0]

    def add_step(cs):
        nonlocal last
        tie(stages[cs][0], last)
        stages[cs] = add_stages(*stages[cs])
        last = stages[cs][0]

    def sum_step(cs):
        nonlocal last
        tie(stages[cs][0], last)
        last = sum_chunks(cs, *stages[cs])

    def got_step(c):
        nonlocal last
        tie(last, got[c])

    def forward_step(c):
        tie(kept[2], last)
        kept[3] = Box(over_col(kept[2].value, 1))

    steps = {
        "s": send_step,
        "p": place_step,
        "k": keep_step,
        "a": add_step,
        "u": sum_step,
        "g": got_step,
        "f": forward_step,
    }
    for kind, what in STEPS:
        steps[kind](what)
    parts, places = [], []
    for (piece, start, count), spans in zip(order, where, strict=True):
        if spans[0][0] == 2 and piece == 3:
            part = over_col(parts[-1][:, widths[2] - count :], 1)
        elif spans[0][0] == 2:
            part = over_col(sums[2][0].value, piece)
        else:
            spans = [(sums[c][0].value, sums[c][1] + s, n) for c, s, n in spans]
            part = jnp.concatenate([total[:, s : s + n] for total, s, n in spans], axis=1)
            part = over_col(part, piece) if piece else part
        parts.append(part)
        places.append((piece, start, count))
    out = kernel_call(
        functools.partial(finish, places),
        like((n_pair, block, piece_rows), F32),
        (ids, *parts),
        scratch=[pltpu.VMEM((n_pair, block, piece_rows), F32), pltpu.SemaphoreType.DMA((n_pair,))],
        name="finish",
        out_spec=HBM,
    )
    return out.transpose(0, 2, 1)


def solution(mesh):
    placed = (
        P(None, ("row", "col"), None),
        P("row", "col", None),
        P("row", None, None),
        P(),
        P(),
        P(),
    )
    return jax.shard_map(
        functools.partial(local, mesh.shape["row"], mesh.shape["col"]),
        mesh=mesh,
        in_specs=placed,
        out_specs=P(None, "col", "row"),
        check_vma=False,
    )
```

```python
import functools

import jax
import jax.numpy as jnp
from jax import lax
from jax.experimental import pallas as pl
from jax.experimental.pallas import tpu as pltpu
from jax.sharding import PartitionSpec as P

TILE = 64
BF = jnp.bfloat16
F32 = jnp.float32
VMEM = pl.BlockSpec(memory_space=pltpu.VMEM)
SMEM = pl.BlockSpec(memory_space=pltpu.SMEM)
HBM = pl.BlockSpec(memory_space=pltpu.HBM)
LIMIT = 10 * 2**20
COL, LOW, HIGH, ROW = range(4)
ROWS_AT, PIECES_AT, KEPT_AT = (1, 0), (1, 1), (1, 0)
STEPS = (
    ("s", 0),
    ("s", 1),
    ("g", 0),
    ("f", 0),
    ("p", 2),
    ("p", 3),
    ("s", 2),
    ("k", (0, 1)),
    ("s", 3),
    ("k", (2,)),
    ("a", (0, 1)),
    ("a", (2,)),
    ("k", (3,)),
    ("u", (0, 1)),
    ("u", (2,)),
    ("u", (3,)),
)


def kernel_call(body, outs, ins, scratch=(), name=None, out_spec=VMEM, aliases=None):
    return pl.pallas_call(
        body,
        out_shape=outs,
        in_specs=[SMEM] + [VMEM] * (len(ins) - 1),
        out_specs=jax.tree.map(lambda _: out_spec, outs),
        scratch_shapes=scratch,
        compiler_params=pltpu.CompilerParams(vmem_limit_bytes=LIMIT),
        cost_estimate=pl.CostEstimate(flops=0, bytes_accessed=0, transcendentals=0),
        input_output_aliases=aliases or {},
        name=name,
    )(*ins)


def like(shape, dtype):
    return jax.ShapeDtypeStruct(shape, dtype)


class Box:
    def __init__(self, value):
        self.value = value


def tie(*boxes):
    values = lax.optimization_barrier(tuple(box.value for box in boxes))
    for box, value in zip(boxes, values, strict=True):
        box.value = value


def iota(shape, dim):
    return lax.broadcasted_iota(jnp.int32, shape, dim)


def spread(row_tiles, tiles, size):
    count = tiles.shape[0]
    picker = (row_tiles == iota((row_tiles.shape[0], count), 1)).astype(F32).astype(BF)
    wide = (iota((count, size), 1) // TILE == iota((count, size), 0)).astype(F32).astype(BF)
    rows = jnp.dot(picker, tiles.astype(F32).astype(BF), preferred_element_type=F32).astype(BF)
    return jnp.dot(rows, wide, preferred_element_type=F32).astype(BF)


def mask_slab(n_col, ks, ids, tiles, *refs):
    pieces, out = refs[:-1], refs[-1]
    rows, size = pieces[0].shape
    for k, piece in zip(ks, pieces, strict=True):
        owner = ids[COL] ^ k
        row_tiles = ((ids[ROW] * n_col + owner) * rows + iota((rows, 1), 0)) // TILE
        out[owner % 2] = piece[...] * spread(row_tiles, tiles[...], size)


def place_blocks(places, ids, *refs):
    for place, block in zip(places, refs, strict=False):
        refs[-1][place(ids)] = block[...]


def masked_block(ids, tiles, piece, group, half, groups, block, size):
    first = ((piece * groups + group) * 2 + half) * block
    return spread((first + iota((block, 1), 0)) // TILE, tiles[...], size)


def place_pieces(ks, ids, tiles, *refs):
    pieces, (other, kept) = refs[: len(ks)], refs[len(ks) :]
    for k, piece in zip(ks, pieces, strict=True):
        aux, groups, _, block, size = piece.shape
        owner = ids[COL] ^ k
        for half, out in ((1 - ids[LOW], other), (ids[LOW], kept)):
            for g in range(groups):
                mask = masked_block(ids, tiles, owner, g, half, groups, block, size)
                for q in range(aux):
                    out[q, owner * groups + g] = piece[q, g, half] * mask


def place_halves(ks, other_half, ids, tiles, *refs):
    pieces, out = refs[: len(ks)], refs[-1]
    half = 1 - ids[LOW] if other_half else ids[LOW]
    for k, piece in zip(ks, pieces, strict=True):
        aux, groups, block, size = piece.shape
        owner = ids[COL] ^ k
        for g in range(groups):
            mask = masked_block(ids, tiles, owner, g, half, groups, block, size)
            for q in range(aux):
                out[q, owner * groups + g] = piece[q, g] * mask


def place_parts(k, ids, tiles, *refs):
    out = refs[-1]
    pieces = refs[: out.shape[0]]
    owner = ids[COL] ^ k
    _, groups, block, size = pieces[0].shape
    for g in range(groups):
        mask = masked_block(ids, tiles, owner, g, 1 - ids[LOW], groups, block, size)
        for q, piece in enumerate(pieces):
            out[q, owner * groups + g] = piece[0, g] * mask


def multiply_rows(factors, inter, carried, first, width):
    value = jnp.dot(carried[...], first[...], preferred_element_type=F32)
    for q in range(factors.shape[0]):
        value += lax.dot_general(
            factors[q],
            inter[pl.ds(q * width, width), :],
            (((1,), (1,)), ((), ())),
            preferred_element_type=F32,
        )
    return value


def runs(segments, block):
    found, to = [], 0
    for piece, start, count in segments:
        end = start + count
        while start < end:
            group, half, at = start // (2 * block), start // block % 2, start % block
            n = min(block - at, end - start)
            found.append((piece, group, half, at, n, to))
            start, to = start + n, to + n
    return found


def pick_rows(segments, width, ids, other, kept, picked):
    aux, n_high, block, _ = other.shape
    groups = max(1, n_high // 4)
    for low in range(2):

        @pl.when(ids[LOW] == low)
        def _():
            for piece, group, half, at, n, to in runs(segments, block):
                source = kept if half == low else other
                for q in range(aux):
                    picked[q * width + to : q * width + to + n, :] = source[
                        q, (ids[COL] ^ piece) * groups + group, at : at + n, :
                    ]


def times_amplitudes(picked, amp, inter, more=None):
    size = amp.shape[1]
    step = 256 if size % 256 == 0 else size
    rows = inter.shape[0]
    for i in range(size // step):
        at = slice(i * step, (i + 1) * step)
        value = jnp.dot(picked[...], amp[:, at], preferred_element_type=F32)
        inter[:, at] = value[:rows].astype(BF)
        if more is not None:
            more[:, at] = value[rows:]


def first_send_part(segments, width, ids, *refs):
    others, kepts, amp, factors, second, first, inter, send, other, kept, picked, rows, turned = refs
    aux = factors.shape[0]
    block = send.shape[1]
    pick_rows(segments, width, ids, others, kepts, picked)
    picked[aux * width :, :] = second[...]

    @pl.when(ids[LOW] >= 0)
    def _():
        times_amplitudes(picked, amp, inter, rows)

    @pl.when(ids[LOW] >= 0)
    def _():
        u = rows[...]
        high = u.astype(BF).astype(F32)
        turned[...] = jnp.concatenate([high[:aux], (u - high)[:aux]], axis=0).T
        for h in range(send.shape[0]):
            for half, out in ((1 - ids[LOW], other), (ids[LOW], kept)):
                at = pl.ds(pl.multiple_of((2 * h + half) * block, 8), block)
                out[h * block : (h + 1) * block, :] = turned[at, :].astype(BF)

    @pl.when(ids[LOW] >= 0)
    def _():
        value = multiply_rows(factors, inter, other, first, width)
        for h in range(send.shape[0]):
            send[h] = value[h * block : (h + 1) * block, :].astype(BF)


def send_part(segments, width, ids, *refs):
    others, kepts, amp, factors, carried, first, inter, send, picked = refs
    block = send.shape[1]
    pick_rows(segments, width, ids, others, kepts, picked)

    @pl.when(ids[LOW] >= 0)
    def _():
        times_amplitudes(picked, amp, inter)

    @pl.when(ids[LOW] >= 0)
    def _():
        value = multiply_rows(factors, inter, carried, first, width)
        for h in range(send.shape[0]):
            send[h] = value[h * block : (h + 1) * block, :].astype(BF)


def keep_rows(widths, ids, factors, carried, *refs):
    count = len(widths)
    inter, first, got = refs[:count], refs[count : 2 * count], refs[2 * count : 3 * count]
    total = refs[-1]
    block = got[0].shape[1]

    def part(c, at, width):
        @pl.when(ids[LOW] >= 0)
        def _():
            value = multiply_rows(factors, inter[c], carried, first[c], width)
            for h in range(got[c].shape[0]):
                total[h, :, at : at + width] = value[h * block : (h + 1) * block, :] + got[c][h].astype(F32)

    for c, width in enumerate(widths):
        part(c, sum(widths[:c]), width)
    return refs[3 * count : -1], total


def keep_direct(widths, ids, *refs):
    (own, *messages), total = keep_rows(widths, ids, *refs)
    own[...] = total[ids[HIGH]]
    for k, message in enumerate(messages, 1):
        message[...] = total[ids[HIGH] ^ k].astype(BF)


def keep_halves(widths, ids, *refs):
    (mine, message), total = keep_rows(widths, ids, *refs)
    for i in range(mine.shape[0]):
        mine[i] = total[ids[HIGH] ^ (2 * i)]
        message[i] = total[ids[HIGH] ^ (2 * i + 1)].astype(BF)


def add_halves(ids, mine, got, kept, message):
    for i in range(kept.shape[0]):
        kept[i] = mine[2 * i] + got[2 * i].astype(F32)
        message[i] = (mine[2 * i + 1] + got[2 * i + 1].astype(F32)).astype(BF)


def add_up(ids, own, *refs):
    value = own[...]
    for got in refs[:-1]:
        value += got[...].astype(F32)
    refs[-1][...] = value


def finish(places, ids, *refs):
    parts, out, whole, sems = refs[:-3], refs[-3], refs[-2], refs[-1]
    copies = []
    for k in range(whole.shape[0]):
        found = [(place, part) for place, part in zip(places, parts, strict=True) if place[0] == k]
        source = whole.at[k]
        if len(found) == 1 and found[0][1].shape == source.shape:
            source = found[0][1]
        else:
            for (_, start, count), part in found:
                whole[k, :, start : start + count] = part[:, :count]
        copy = pltpu.make_async_copy(source, out.at[ids[COL] ^ k], sems.at[k])
        copy.start()
        copies.append(copy)
    for copy in copies:
        copy.wait()


def local(n_row, n_col, amplitudes, integrals, occupied, pairs, amp_tiles, int_tiles):
    n_pair, chunk_rows, size = amplitudes.shape
    aux, piece_rows, _ = integrals.shape
    n_high = n_row // 2
    block = size // n_row
    groups = piece_rows // (2 * block)
    half_size = n_high * block
    col, row = lax.axis_index("col"), lax.axis_index("row")
    ids = jnp.stack([col, row % 2, row // 2, row]).astype(jnp.int32)

    def over_col(x, k):
        return lax.ppermute(x, "col", [(i, i ^ k) for i in range(n_col)])

    def over_low(x):
        return lax.ppermute(x, "row", [(i, i ^ 1) for i in range(n_row)])

    def over_high(x, k):
        return lax.ppermute(x, "row", [(i, (i // 2 ^ k) * 2 + i % 2) for i in range(n_row)])

    def up(x):
        return lax.ppermute(x, "row", [(i, (i + 2) % n_row) for i in range(n_row)])

    mine = [lax.dynamic_index_in_dim(amplitudes, col ^ k, 0, keepdims=False) for k in range(n_col)]
    mine = [Box(mine[0])] + [Box(over_col(mine[k], k)) for k in range(1, n_col)]
    split = integrals.reshape(aux, groups, 2, block, size)
    low = row % 2
    other, kept = {}, {}
    split1 = Box(over_col(integrals, 1))
    tie(split1, mine[1])
    split_other, split_kept = Box(split), Box(split)

    def half_rows(box, half):
        return Box(lax.dynamic_index_in_dim(box.value, half, 2, keepdims=False))

    is_col = jnp.arange(n_pair, dtype=jnp.int32) == col
    pair_tiles = Box(jnp.sum(jnp.where(is_col[:, None, None], amp_tiles, 0), axis=0))
    tie(pair_tiles, mine[1])

    pair = jnp.sum(jnp.where(is_col[:, None], pairs, 0), axis=0)
    orbitals = jnp.arange(occupied.shape[1], dtype=jnp.int32)
    picks = (pair[:, None] == orbitals[None, :]).astype(BF)
    rows = jnp.einsum("po,qov->pqv", picks, occupied, preferred_element_type=F32).astype(BF)
    first, second = rows[0], rows[1]
    second = jnp.concatenate([second, jnp.zeros((16 - aux, size), BF)], axis=0)
    first = first.reshape(aux, n_col, piece_rows)
    first = [lax.dynamic_index_in_dim(first, col ^ k, 1, keepdims=False) for k in range(n_col)]
    first = [jnp.concatenate([x, x], axis=0) for x in first]

    step = min(256, piece_rows)
    widths = [step, 2 * piece_rows - step, 2 * piece_rows - step, step]
    cut = max(piece_rows - widths[-1], 0)
    order = [(1, 0, piece_rows), (0, 0, piece_rows), (2, 0, piece_rows), (3, 0, cut), (3, cut, piece_rows - cut)]
    order = [part for part in order if part[2]]
    chunks, where = [[] for _ in widths], []
    at = 0
    for piece, start, count in order:
        spans = []
        while count:
            done = sum(n for _, _, n in chunks[at])
            n = min(count, widths[at] - done)
            chunks[at].append((piece, start, n))
            spans.append((at, done, n))
            start, count = start + n, count - n
            at += done + n == widths[at]
        where.append(spans)
    first = [jnp.concatenate([first[p][:, s : s + n] for p, s, n in chunk], axis=1) for chunk in chunks]

    second, first = Box(second), [Box(x) for x in first]

    def half_slab(ks):
        return kernel_call(
            functools.partial(mask_slab, n_col, ks),
            like((2, chunk_rows, size), BF),
            (ids, pair_tiles.value, *[mine[k].value for k in ks]),
            name="half_slab",
        ).reshape(2 * chunk_rows, size)

    shape = like((aux, n_high, block, size), BF)
    all_other, all_kept = map(
        Box,
        kernel_call(
            functools.partial(place_pieces, (0, 1)),
            (shape, shape),
            (ids, int_tiles, split, split1.value.reshape(split.shape)),
            name="place_pieces",
        ),
    )

    def place(pieces, k, into, other_half):
        return kernel_call(
            functools.partial(place_halves, (k,), other_half),
            shape,
            (ids, int_tiles, pieces[k].value, into.value),
            aliases={3: 0},
            name="place_halves",
        )

    def flat(x):
        return x.reshape(aux, half_size, size)

    def slab_place(step, other_low, side, ids):
        h = lax.rem(ids[HIGH] + (n_high - step), n_high)
        low = 1 - ids[LOW] if other_low else ids[LOW]
        return (h * 2 + low) * 2 + (ids[COL] // 2 ^ side)

    def place_slabs(found):
        places = [functools.partial(slab_place, *place) for _, place in found]
        return kernel_call(
            functools.partial(place_blocks, places),
            like((n_row * 2, 2 * chunk_rows, size), BF),
            (ids, *[slab.value for slab, _ in found]),
            name="place_rows",
        )

    rings = [[Box(half_slab((0, 1)))]]
    tie(split_other, rings[0][0])
    send_other = half_rows(split_other, 1 - low)
    other[2] = Box(over_col(send_other.value, 2))
    swapped = [[], []]

    def hop(r, s):
        nonlocal send_kept
        ring = rings[r]
        if s > 0 and not (s == n_high - 1 and r == 1):
            tie(ring[s], swapped[r][-1])
        if (s, r) == ROWS_AT:
            tie(ring[s], second, *first)
        if (s, r) == PIECES_AT:
            tie(ring[s], all_other, all_kept)
        if (s, r) == KEPT_AT:
            tie(ring[s], split_kept)
            send_kept = half_rows(split_kept, low)
            tie(ring[s], send_kept)
        if s + 1 < n_high:
            ring.append(Box(up(ring[s].value)))
        if s == n_high - 1 and r == 1:
            swapped[r].append(Box(up(swapped[r][-1].value)))
        else:
            swapped[r].append(Box(over_low(ring[s].value)))

    send_kept = None
    tie(rings[0][0], mine[2], mine[3])
    rings.append([Box(half_slab((2, 3)))])
    for s in range(n_high):
        hop(0, s)
        hop(1, s)
    tie(other[2], rings[0][-1], rings[1][-1], swapped[1][-2])
    other[3] = [over_col(other[2].value[q : q + 1], 1) for q in range(aux)]
    kept[2] = Box(over_col(send_kept.value, 2))
    all_other = Box(place(other, 2, all_other, True))
    found = [(slab, (s, low, r)) for low, side in enumerate((rings, swapped)) for r in range(2) for s, slab in enumerate(side[r])]
    amp = Box(place_slabs(found).reshape(size, size))
    all_other = Box(
        kernel_call(
            functools.partial(place_parts, 3),
            shape,
            (ids, int_tiles, *other[3], all_other.value),
            aliases={2 + aux: 0},
            name="place_parts",
        )
    )

    inter, got, sums, carried = {}, {}, {}, []

    def send_chunk(c):
        pieces = (all_other.value, all_kept.value)
        width = widths[c]
        outs = (like((aux * width, size), BF), like((n_high, block, width), BF))
        if not carried:
            extra = second.value.shape[0]
            x, send, *terms = kernel_call(
                functools.partial(first_send_part, chunks[c], width),
                outs + (like((half_size, 2 * aux), BF),) * 2,
                (ids, *pieces, amp.value, flat(all_other.value), second.value, first[c].value),
                scratch=[
                    pltpu.VMEM((aux * width + extra, size), BF),
                    pltpu.VMEM((extra, size), F32),
                    pltpu.VMEM((size, 2 * aux), F32),
                ],
                name="send_part",
            )
            carried.extend(terms)
        else:
            x, send = kernel_call(
                functools.partial(send_part, chunks[c], width),
                outs,
                (ids, *pieces, amp.value, flat(all_other.value), carried[0], first[c].value),
                scratch=[pltpu.VMEM((aux * width, size), BF)],
                name="send_part",
            )
        inter[c] = Box(x)
        send = Box(send)
        tie(send)
        got[c] = Box(over_low(send.value))

    def keep_chunks(cs, direct=False):
        own_widths = tuple(widths[c] for c in cs)
        wide = sum(own_widths)
        half = n_high // 2
        if direct:
            body, outs = keep_direct, (like((block, wide), F32),) + (like((block, wide), BF),) * (n_high - 1)
        else:
            body, outs = keep_halves, (like((half, block, wide), F32), like((half, block, wide), BF))
        own, *messages = kernel_call(
            functools.partial(body, own_widths),
            outs,
            (ids, flat(all_kept.value), carried[1])
            + tuple(inter[c].value for c in cs)
            + tuple(first[c].value for c in cs)
            + tuple(got[c].value for c in cs),
            scratch=[pltpu.VMEM((n_high, block, wide), F32)],
            name="keep_part",
        )
        if direct:
            messages = [Box(over_high(m, k)) for k, m in enumerate(messages, 1)]
        else:
            messages = [Box(over_high(messages[0], 1))]
        return Box(own), messages

    def add_stages(own, messages):
        step = 2
        while own.value.shape[0] > 1:
            half = own.value.shape[0] // 2
            shape = (half,) + own.value.shape[1:]
            mine, message = kernel_call(
                add_halves, (like(shape, F32), like(shape, BF)), (ids, own.value, messages[0].value), name="add_halves"
            )
            own, messages = Box(mine), [Box(over_high(message, step))]
            step *= 2
        return own, messages

    def sum_chunks(cs, own, messages):
        shape = (block, sum(widths[c] for c in cs))
        total = kernel_call(
            add_up,
            like(shape, F32),
            (ids, own.value.reshape(shape), *[m.value.reshape(shape) for m in messages]),
            name="add_up",
        )
        total = Box(total)
        at = 0
        for c in cs:
            sums[c] = (total, at)
            at += widths[c]
        return total

    stages = {}
    last = amp

    def send_step(c):
        nonlocal last
        if c:
            tie(amp, last)
        send_chunk(c)
        last = inter[c]

    def place_step(k):
        nonlocal last, all_kept
        tie(all_kept, last)
        all_kept = Box(place(kept, k, all_kept, False))
        last = all_kept

    def keep_step(cs):
        nonlocal last
        tie(inter[cs[-1]], last)
        stages[cs] = keep_chunks(cs, direct=cs == (3,))
        last = stages[cs][0]

    def add_step(cs):
        nonlocal last
        tie(stages[cs][0], last)
        stages[cs] = add_stages(*stages[cs])
        last = stages[cs][0]

    def sum_step(cs):
        nonlocal last
        tie(stages[cs][0], last)
        last = sum_chunks(cs, *stages[cs])

    def got_step(c):
        nonlocal last
        tie(last, got[c])

    def forward_step(c):
        tie(kept[2], last)
        kept[3] = Box(over_col(kept[2].value, 1))

    steps = {
        "s": send_step,
        "p": place_step,
        "k": keep_step,
        "a": add_step,
        "u": sum_step,
        "g": got_step,
        "f": forward_step,
    }
    for kind, what in STEPS:
        steps[kind](what)
    parts, places = [], []
    for (piece, start, count), spans in zip(order, where, strict=True):
        if spans[0][0] == 2 and piece == 3:
            part = over_col(parts[-1][:, widths[2] - count :], 1)
        elif spans[0][0] == 2:
            part = over_col(sums[2][0].value, piece)
        else:
            spans = [(sums[c][0].value, sums[c][1] + s, n) for c, s, n in spans]
            part = jnp.concatenate([total[:, s : s + n] for total, s, n in spans], axis=1)
            part = over_col(part, piece) if piece else part
        parts.append(part)
        places.append((piece, start, count))
    out = kernel_call(
        functools.partial(finish, places),
        like((n_pair, block, piece_rows), F32),
        (ids, *parts),
        scratch=[pltpu.VMEM((n_pair, block, piece_rows), F32), pltpu.SemaphoreType.DMA((n_pair,))],
        name="finish",
        out_spec=HBM,
    )
    return out.transpose(0, 2, 1)


def solution(mesh):
    placed = (
        P(None, ("row", "col"), None),
        P("row", "col", None),
        P("row", None, None),
        P(),
        P(),
        P(),
    )
    return jax.shard_map(
        functools.partial(local, mesh.shape["row"], mesh.shape["col"]),
        mesh=mesh,
        in_specs=placed,
        out_specs=P(None, "col", "row"),
        check_vma=False,
    )
```
